32 devices in a mesh: fsdp: 4 (over z), tp: 4 (over y, core), rep: 2 (over x).
Axes of the slice: x: 2, y: 2, z: 4, core: 2. Of those that a mesh axis runs over, the one named last changes fastest.
Arguments:
- hidden: bfloat16 [1024, 16384], P(('rep', 'fsdp')), parts along dimension 0, may hold values from -400 to 400
- base_weight: bfloat16 [32768, 16384], P(('rep', 'fsdp', 'tp')), parts along dimension 0, may hold values from -1 to 1
- adapter_down: bfloat16 [32768, 32], P(('rep', 'fsdp', 'tp')), parts along dimension 0, may hold values from -0.046875 to 0.046875
- adapter_up: bfloat16 [64, 16384], P('rep'), parts along dimension 0, may hold values from -0.1796875 to 0.1796875
- norm_gain: bfloat16 [32768], P('rep'), parts along dimension 0, may hold values from 0.25 to 1.75
- positions: int32 [1024], P(('rep', 'fsdp')), parts along dimension 0, may hold values from 0 to 4606, as said below
Outputs:
- queries: bfloat16 [1024, 16384], P(('rep', 'fsdp'), 'tp'), parts along dimension 0
The draws below stay inside these ranges and needn't reach their ends.
There are 2 independent parts, one for each index of `rep`. The reference program is written for one: setup_inputs(seed, part) draws one part's arguments, and reference() takes and returns one part's arrays. A program takes and returns all parts, laid end to end along the dimension named above; each array names one. Nothing has to cross between parts.
Inputs may be any that keep to these rules, and one draw needn't show every extreme that they name: Within a document positions rise by one from token to token; every document after the first starts at 0; the first document continues an earlier one and its last token has position 4606.
All inputs are finite; a program needn't handle non-finite values.
Results may differ from the reference program's by a relative error of at most 0.018.
Values may be sent and summed in bfloat16 or wider, within the bound.
No kernel may reach another device: no remote copies, remote signals or barrier semaphores. Data moves between devices by JAX's collectives and lax.ppermute only.
A program may use at most 320 MiB of HBM per device.

```python
import math
import jax
import jax.numpy as jnp
from jax import lax

D = 16384
HEAD = 128
R = 32
BLOCK = 128
TOKENS = 512
N_FSDP = 4


def draw_hidden(key, part):
    noise_key, row_key, col_key = jax.random.split(key, 3)
    row_scale = jnp.exp(jax.random.uniform(row_key, (TOKENS, 1), jnp.float32, 0.0, math.log(10.0)))
    col_scale = jnp.exp(jax.random.uniform(col_key, (1, D), jnp.float32, 0.0, math.log(10.0)))
    noise = jnp.clip(jax.random.normal(noise_key, (TOKENS, D), jnp.float32), -4.0, 4.0)
    return (noise * row_scale * col_scale).astype(jnp.bfloat16)


def draw_base_weight(key, part):
    noise_key, row_key, col_key = jax.random.split(jax.random.fold_in(key, 7), 3)
    row_factor = jnp.exp(jax.random.uniform(row_key, (D, 1), jnp.float32, math.log(0.2), math.log(2.0)))
    col_factor = jnp.exp(jax.random.uniform(col_key, (1, D), jnp.float32, math.log(0.2), math.log(2.0)))
    noise = jnp.clip(jax.random.normal(noise_key, (D, D), jnp.float32), -4.0, 4.0)
    return (noise * row_factor * col_factor * (1.0 / math.sqrt(D))).astype(jnp.bfloat16)


def draw_positions(key, part):
    start_key, forced_key = jax.random.split(jax.random.fold_in(key, 13), 2)
    index = jnp.arange(TOKENS, dtype=jnp.int32)
    spacing = max(4, TOKENS // 8)
    forced = jax.random.randint(forced_key, (), 1, TOKENS, dtype=jnp.int32)
    starts = (jax.random.randint(start_key, (TOKENS,), 0, spacing, dtype=jnp.int32) == 0) | (index == 0) | (index == forced)
    latest = lax.cummax(jnp.where(starts, index, 0), axis=0)
    later = starts & (index > 0)
    first_length = jnp.min(jnp.where(later, index, TOKENS)).astype(jnp.int32)
    offset = (TOKENS + 4095 - first_length).astype(jnp.int32)
    return (index - latest + jnp.where(latest == 0, offset, 0)).astype(jnp.int32)


def levels(stream_key, shape, cuts, low, high):
    factor_of, own = 1.0, jax.random.fold_in(stream_key, 6)
    for position, blocks in cuts:
        heights = jnp.exp(jax.random.uniform(jax.random.fold_in(own, position), (blocks,), jnp.float32, low / len(cuts), high / len(cuts)))
        factor_of = factor_of * jnp.repeat(heights, shape[position] // blocks).reshape([-1 if axis == position else 1 for axis in range(len(shape))])
    return factor_of


def normal_values(key, dims, scale, limit, shards=(), kind=jnp.bfloat16):
    gain = levels(key, dims, shards, -0.22, 0.18) if shards else 1.0
    drawn = jax.random.normal(key, dims, jnp.float32) * scale * gain
    return jnp.minimum(jnp.maximum(drawn, -limit), limit).astype(kind)


def setup_inputs(seed: int = 0, part: int = 0) -> dict:
    keys = jax.random.split(jax.random.key(seed), 7)
    part_keys = jax.random.split(jax.random.fold_in(keys[6], part), 7)
    hidden = draw_hidden(jax.random.fold_in(jax.random.fold_in(keys[6], part), 71), part)
    base_weight = draw_base_weight(jax.random.fold_in(jax.random.fold_in(keys[6], part), 71), part)
    adapter_down = normal_values(part_keys[2], (D, R), D ** -0.5, 0.046875, ((0, 16),))
    adapter_up = normal_values(part_keys[3], (R, D), 0.03, 0.1796875)
    norm_gain = jnp.clip(1.0 + 0.15 * jax.random.normal(part_keys[4], (D,), jnp.float32), 0.25, 1.75).astype(jnp.bfloat16)
    positions = draw_positions(jax.random.fold_in(jax.random.fold_in(keys[6], part), 71), part)
    return {"hidden": hidden, "base_weight": base_weight, "adapter_down": adapter_down, "adapter_up": adapter_up, "norm_gain": norm_gain, "positions": positions}


norm_epsilon = 1e-05
scale_epsilon = 1e-06
code_limit = 15.0
adapter_scale = 2.0
rope_theta = 500000.0
rope_factor = 8.0
low_factor = 1.0
high_factor = 4.0
initial_context = 8192.0

def normalize(hidden, norm_gain):
    values = hidden.astype(jnp.float32)
    mean_square = lax.optimization_barrier(jnp.mean(values * values, axis=1, keepdims=True))
    return (values * lax.rsqrt(mean_square + norm_epsilon) * norm_gain.astype(jnp.float32)[None, :]).astype(jnp.bfloat16)

def quantize(base_rows, low_rank):
    merged = base_rows.astype(jnp.float32) + adapter_scale * low_rank
    row_count, col_count = merged.shape
    tiles = merged.reshape(row_count // BLOCK, BLOCK, col_count // BLOCK, BLOCK)
    largest = lax.optimization_barrier(jnp.max(jnp.abs(tiles), axis=(1, 3)))
    exponent = jnp.ceil(jnp.log2((largest + scale_epsilon) / code_limit))
    scales = jnp.exp2(exponent).astype(jnp.bfloat16)
    quantized = jnp.floor(tiles / scales.astype(jnp.float32)[:, None, :, None] + 0.5).astype(jnp.bfloat16)
    return (quantized.reshape(row_count, col_count), scales)

def dequantize(quantized, scales):
    row_count, col_count = quantized.shape
    tiles = quantized.reshape(row_count // BLOCK, BLOCK, col_count // BLOCK, BLOCK).astype(jnp.float32)
    return (tiles * scales.astype(jnp.float32)[:, None, :, None]).astype(jnp.bfloat16).reshape(row_count, col_count)

def frequencies(positions):
    pair_index = jnp.arange(HEAD // 2, dtype=jnp.float32)
    inverse = jnp.exp(pair_index * (-2.0 * math.log(rope_theta) / HEAD))
    wavelength = 2.0 * math.pi / inverse
    blend = (initial_context / wavelength - low_factor) / (high_factor - low_factor)
    middle = (1.0 - blend) * inverse / rope_factor + blend * inverse
    adjusted = jnp.where(wavelength < initial_context / high_factor, inverse, jnp.where(wavelength > initial_context / low_factor, inverse / rope_factor, middle))
    angles = positions.astype(jnp.float32)[:, None] * adjusted[None, :]
    return (jnp.cos(angles), jnp.sin(angles))

def rotate(projected, positions):
    cosine, sine_part = frequencies(positions)
    row_count, full_width = projected.shape
    half_head = HEAD // 2
    per_head = projected.reshape(row_count, full_width // HEAD, HEAD)
    first_half = per_head[:, :, :half_head]
    second_half = per_head[:, :, half_head:]
    cosine = cosine[:, None, :]
    sine_part = sine_part[:, None, :]
    turned = jnp.concatenate([first_half * cosine - second_half * sine_part, second_half * cosine + first_half * sine_part], axis=2)
    return turned.reshape(row_count, full_width)

def reference(hidden, base_weight, adapter_down, adapter_up, norm_gain, positions):
    normed = normalize(hidden, norm_gain)
    group_rows = D // N_FSDP

    def one_group(carry, group_index):
        first_row = (group_index * group_rows).astype(jnp.int32)
        base_rows = lax.dynamic_slice_in_dim(base_weight, first_row, group_rows, 0)
        down_rows = lax.dynamic_slice_in_dim(adapter_down, first_row, group_rows, 0)
        input_cols = lax.dynamic_slice_in_dim(normed, first_row, group_rows, 1)
        low_rank = jnp.dot(down_rows, adapter_up, preferred_element_type=jnp.float32)
        quantized, scales = quantize(base_rows, low_rank)
        weight = dequantize(quantized, scales)
        partial_value = jnp.dot(input_cols, weight, preferred_element_type=jnp.float32)
        partial_value = lax.optimization_barrier(partial_value.astype(jnp.bfloat16)).astype(jnp.float32)
        return (carry + partial_value, None)
    projected, _ = lax.scan(one_group, jnp.zeros((TOKENS, D), jnp.float32), jnp.arange(N_FSDP, dtype=jnp.int32))
    return rotate(projected, positions).astype(jnp.bfloat16)
```

```python
import functools
import math

import jax
import jax.numpy as jnp
from jax import lax
from jax.experimental import pallas as pl
from jax.experimental.pallas import tpu as pltpu
from jax.sharding import PartitionSpec as P

HEAD = 128
BLOCK = 128
CHUNKS = 4


norm_epsilon = 1e-05
scale_epsilon = 1e-06
code_limit = 15.0
adapter_scale = 2.0
rope_theta = 500000.0
rope_factor = 8.0
low_factor = 1.0
high_factor = 4.0
initial_context = 8192.0
feature_scale = 1024.0

VMEM_LIMIT = 48 << 20
ANY = pl.BlockSpec(memory_space=pl.ANY)


def params():
    return pltpu.CompilerParams(vmem_limit_bytes=VMEM_LIMIT)


def cost(flops, nbytes):
    return pl.CostEstimate(flops=int(flops), bytes_accessed=int(nbytes), transcendentals=0)


def like(shape, dtype=jnp.bfloat16):
    return jax.ShapeDtypeStruct(shape, dtype)


def frequencies(positions):
    pair_index = jnp.arange(HEAD // 2, dtype=jnp.float32)
    inverse = jnp.exp(pair_index * (-2.0 * math.log(rope_theta) / HEAD))
    wavelength = 2.0 * math.pi / inverse
    blend = (initial_context / wavelength - low_factor) / (high_factor - low_factor)
    middle = (1.0 - blend) * inverse / rope_factor + blend * inverse
    adjusted = jnp.where(
        wavelength < initial_context / high_factor,
        inverse,
        jnp.where(wavelength > initial_context / low_factor, inverse / rope_factor, middle),
    )
    angles = positions.astype(jnp.float32)[:, None] * adjusted[None, :]
    return (jnp.cos(angles), jnp.sin(angles))


def turn_tables(hidden, positions):
    values = hidden.astype(jnp.float32)
    mean_square = jnp.mean(values * values, axis=1, keepdims=True)
    factor = lax.rsqrt(mean_square + norm_epsilon) * (1.0 / feature_scale)
    cosine, sine_part = frequencies(positions)
    return (
        jnp.concatenate([cosine, cosine], axis=1) * factor,
        jnp.concatenate([-sine_part, sine_part], axis=1) * factor,
    )


def pick_kernel(table, *refs):
    count = len(refs) // 3
    for i in range(count):
        values, gain, out = refs[i], refs[count + i], refs[2 * count + i]
        scaled = values[...].astype(jnp.float32) * (gain[...].astype(jnp.float32) * feature_scale)
        out[...] = scaled.astype(jnp.bfloat16)


def pick(hidden, norm_gain, table, count, width):
    tokens = hidden.shape[0]

    def spec(rows, i):
        return pl.BlockSpec((rows, width), lambda step, table: (0, table[i]))

    return pl.pallas_call(
        pick_kernel,
        grid_spec=pltpu.PrefetchScalarGridSpec(
            num_scalar_prefetch=1,
            grid=(1,),
            in_specs=[spec(tokens, i) for i in range(count)] + [spec(1, i) for i in range(count)],
            out_specs=[pl.BlockSpec((tokens, width), lambda step, table: (0, 0))] * count,
        ),
        out_shape=[like((tokens, width))] * count,
        compiler_params=params(),
        name="pick_features",
    )(table, *([hidden] * count), *([norm_gain] * count))


def scales_of(largest):
    ratio = (largest + scale_epsilon) / code_limit
    scale = jnp.exp2(jnp.ceil(jnp.log2(ratio))).astype(jnp.bfloat16).astype(jnp.float32)
    scale = jnp.where(ratio > scale, scale * 2.0, scale)
    return jnp.where(ratio <= scale * 0.5, scale * 0.5, scale)


def quantize_tile(base, down, up, weight, merged, scale_scratch):
    rows, width = base.shape
    row_blocks = rows // BLOCK
    tops = []
    for i in range(row_blocks):
        block_rows = pl.ds(i * BLOCK, BLOCK)
        low_rank = jnp.dot(down[block_rows, :], up[...], preferred_element_type=jnp.float32)
        total = base[block_rows, :].astype(jnp.float32) + low_rank
        merged[block_rows, :] = total
        tops.append(jnp.max(jnp.abs(total), axis=0, keepdims=True))
    top = jnp.concatenate(tops, axis=0)
    for j in range(width // BLOCK):
        cols = slice(j * BLOCK, (j + 1) * BLOCK)
        largest = jnp.max(top[:, cols], axis=1, keepdims=True)
        scale = scales_of(jnp.broadcast_to(largest, (row_blocks, BLOCK)))
        scale_scratch[0, :, cols] = scale
        scale_scratch[1, :, cols] = 1.0 / scale
    for i in range(row_blocks):
        block_rows = pl.ds(i * BLOCK, BLOCK)
        scale = scale_scratch[0, pl.ds(i, 1), :]
        inverse = scale_scratch[1, pl.ds(i, 1), :]
        codes = jnp.floor(merged[block_rows, :] * inverse + 0.5)
        weight[block_rows, :] = codes.astype(jnp.bfloat16) * scale.astype(jnp.bfloat16)


def store_pieces(product, steps_each, parts, outs):
    groups = len(outs) // parts
    tokens = product.shape[0] // parts
    for group in range(groups):

        @pl.when(pl.program_id(0) // steps_each == group)
        def _():
            for i in range(parts):
                outs[group * parts + i][...] = product[i * tokens : (i + 1) * tokens, :]


def piece_specs(tokens, width, steps_each, parts, groups):
    def spec(group):
        first = group * steps_each
        return pl.BlockSpec(
            (tokens // parts, width),
            lambda i, *_: (0, jnp.clip(i - first, 0, steps_each - 1)),
        )

    shape = like((tokens // parts, steps_each * width))
    specs = [spec(group) for group in range(groups) for _ in range(parts)]
    return specs, [shape] * (parts * groups)


def quantize_kernel(steps_each, with_received, table, base, down, up, x, *refs):
    received = refs[0] if with_received else None
    merged, scale_scratch = refs[-2:]
    groups = pl.num_programs(0) // steps_each
    weight, outs = refs[-3 - groups], refs[-2 - groups : -2]
    quantize_tile(base, down, up, weight, merged, scale_scratch)
    product = jnp.dot(x[...], weight[...], preferred_element_type=jnp.float32)
    if with_received:
        product = product + received[...].astype(jnp.float32)
    store_pieces(product.astype(jnp.bfloat16), steps_each, 1, outs)


def quantize_and_project(
    base, down, up, x, table, steps, width, groups=1, received=None, after=()
):
    rows, rank = down.shape
    tokens = x.shape[0]

    def fixed(shape):
        return pl.BlockSpec(shape, lambda i, table: (0, 0))

    def picked(height):
        return pl.BlockSpec((height, width), lambda i, table: (0, table[i]))

    def in_order(height):
        return pl.BlockSpec((height, width), lambda i, table: (0, i))

    in_specs = [picked(rows), fixed((rows, rank)), picked(rank), fixed((tokens, rows))]
    operands = [base, down, up, x]
    if received is not None:
        in_specs.append(in_order(tokens))
        operands.append(received)
    in_specs += [ANY] * len(after)
    operands += after
    piece_blocks, piece_shapes = piece_specs(tokens, width, steps // groups, 1, groups)
    return pl.pallas_call(
        functools.partial(quantize_kernel, steps // groups, received is not None),
        grid_spec=pltpu.PrefetchScalarGridSpec(
            num_scalar_prefetch=1,
            grid=(steps,),
            in_specs=in_specs,
            out_specs=[in_order(rows), *piece_blocks],
            scratch_shapes=[
                pltpu.VMEM((rows, width), jnp.float32),
                pltpu.VMEM((2, rows // BLOCK, width), jnp.float32),
            ],
        ),
        out_shape=[like((rows, steps * width)), *piece_shapes],
        cost_estimate=cost(2 * tokens * rows * steps * width * 4, 4 * rows * steps * width),
        compiler_params=params(),
        name="quantize_and_project",
    )(table, *operands)


def project_kernel(steps_each, parts, groups, with_received, x, weight, *refs):
    received = refs[0] if with_received else None
    product = jnp.dot(x[...], weight[...], preferred_element_type=jnp.float32)
    if with_received:
        product = product + received[...].astype(jnp.float32)
    store_pieces(product.astype(jnp.bfloat16), steps_each, parts, refs[-parts * groups :])


def project(x, weight, steps, parts=1, groups=1, received=None, after=()):
    tokens, rows = x.shape
    width = weight.shape[1] // steps
    in_specs = [
        pl.BlockSpec((tokens, rows), lambda i: (0, 0)),
        pl.BlockSpec((rows, width), lambda i: (0, i)),
    ]
    operands = [x, weight]
    if received is not None:
        in_specs.append(pl.BlockSpec((tokens, width), lambda i: (0, i)))
        operands.append(received)
    in_specs += [ANY] * len(after)
    operands += after
    piece_blocks, piece_shapes = piece_specs(tokens, width, steps // groups, parts, groups)
    return pl.pallas_call(
        functools.partial(project_kernel, steps // groups, parts, groups, received is not None),
        grid=(steps,),
        in_specs=in_specs,
        out_specs=piece_blocks,
        out_shape=piece_shapes,
        cost_estimate=cost(2 * tokens * rows * steps * width, 2 * rows * steps * width),
        compiler_params=params(),
        name="project",
    )(*operands)


def turn_kernel(count, cosine, sine_part, *refs):
    out = refs[-1]
    for j in range(out.shape[1] // HEAD):
        cols = slice(j * HEAD, (j + 1) * HEAD)
        total = refs[0][:, cols].astype(jnp.float32)
        for term in refs[1:count]:
            total = total + term[:, cols].astype(jnp.float32)
        swapped = pltpu.roll(total, HEAD // 2, 1)
        turned = total * cosine[...] + swapped * sine_part[...]
        out[:, cols] = turned.astype(jnp.bfloat16)


def turn(cosine, sine_part, terms, place, places, into):
    tokens, width = terms[0].shape
    whole = pl.BlockSpec((tokens, width), lambda i: (0, 0))
    table = pl.BlockSpec((tokens, HEAD), lambda i: (0, 0))
    extra = [] if into is None else [into]
    count = len(terms)
    return pl.pallas_call(
        functools.partial(turn_kernel, count),
        grid=(1,),
        in_specs=[table] * 2 + [whole] * count + [ANY] * len(extra),
        out_specs=pl.BlockSpec((tokens, width), lambda i: (0, place)),
        out_shape=like((tokens, places * width)),
        input_output_aliases={2 + count: 0} if extra else {},
        compiler_params=params(),
        name="turn",
    )(cosine, sine_part, *terms, *extra)


def added(*terms):
    total = terms[0].astype(jnp.float32)
    for term in terms[1:]:
        total = total + term.astype(jnp.float32)
    return total.astype(jnp.bfloat16)


def tile_width(columns):
    width = min(columns, 1024)
    while columns % width:
        width //= 2
    return width


def line_shards(hidden, base, down, up, norm_gain, positions):
    tp = lax.axis_index("tp")
    z = lax.axis_index("fsdp")
    rows, all_columns = base.shape
    tokens = hidden.shape[0]
    quarter = all_columns // 4
    piece = quarter // CHUNKS
    width = tile_width(piece)
    half = piece // width

    blocks = jnp.stack([((z + d) % 4) * 4 + tp for d in range(4)]).astype(jnp.int32)
    own_x, *others = pick(hidden, norm_gain[None, :], blocks, 4, rows)
    x1, x2, x3 = [
        lax.ppermute(others[d - 1], "fsdp", [(i, (i + d) % 4) for i in range(4)]) for d in (1, 2, 3)
    ]
    low = z < 2
    rest_x = jnp.concatenate([jnp.where(low, x1, x3), x2, jnp.where(low, x3, x1)], axis=0)
    up2 = up * jnp.bfloat16(adapter_scale)
    cosine, sine_part = turn_tables(hidden, positions)

    def tiles(owners, chunk):
        offsets = jnp.arange(half, dtype=jnp.int32) + chunk * half
        tiles_of = quarter // width
        return jnp.concatenate([owner * tiles_of + offsets for owner in owners]).astype(jnp.int32)

    other_core, other_chip, other_both = tp ^ 1, tp ^ 2, tp ^ 3
    over_core = functools.partial(lax.ppermute, axis_name="tp", perm=[(i, i ^ 1) for i in range(4)])
    over_y = functools.partial(lax.ppermute, axis_name="tp", perm=[(i, i ^ 2) for i in range(4)])

    def over_z(values, pairs):
        return lax.ppermute(values, "fsdp", pairs)

    state = {"last": ()}
    own = {}
    rest = {}

    def do_own(chunk):
        weight_a, for_core = quantize_and_project(
            base, down, up2, own_x, tiles((other_both, other_core), chunk), 2 * half, width,
            after=state["last"],
        )
        weight_b, to_send, kept = quantize_and_project(
            base, down, up2, own_x, tiles((other_chip, tp), chunk), 2 * half, width, groups=2,
            received=over_core(for_core),
        )
        state["last"] = (kept,)
        own[chunk] = (weight_a, weight_b, kept, over_y(to_send))

    def do_rest(chunk):
        weight_a, weight_b, _, _ = own[chunk]
        (for_core,) = project(rest_x, weight_a, 2 * half, after=state["last"])
        received = over_core(for_core)
        outs = project(rest_x, weight_b, 2 * half, parts=3, groups=2, received=received)
        state["last"] = (outs[-1],)
        rest[chunk] = (outs[3:], [over_y(value) for value in outs[:3]])

    for chunk in range(2):
        do_own(chunk)
    for chunk in range(2):
        do_rest(chunk)
    for chunk in range(2, CHUNKS):
        do_own(chunk)
        do_rest(chunk)

    out = None
    for chunk in range(CHUNKS):
        (a, b, c), (ya, yb, yc) = rest[chunk]
        first = over_z(added(a, ya), [(0, 1), (3, 2)])
        second = added(b, yb, first)
        right = over_z(second, [(0, 1), (1, 2)])
        left = over_z(second, [(3, 2), (2, 1)])
        far, near = (a, ya), (c, yc)
        to_right = added(*[jnp.where(low, n, f) for f, n in zip(far, near)], right)
        to_left = added(*[jnp.where(low, f, n) for f, n in zip(far, near)], left)
        right = over_z(to_right, [(0, 1), (1, 2), (2, 3)])
        left = over_z(to_left, [(3, 2), (2, 1), (1, 0)])
        _, _, kept, y_kept = own[chunk]
        out = turn(cosine, sine_part, (kept, y_kept, right, left), chunk, CHUNKS, out)
    return out


def any_shards(fsdp, tp_size, hidden, base, down, up, norm_gain, positions):
    tp = lax.axis_index("tp")
    rows, all_columns = base.shape
    tokens = hidden.shape[0]
    share = all_columns // tp_size
    chunks = max(1, share // 256)
    piece = share // chunks
    width = tile_width(piece)
    steps = piece // width

    blocks = (jnp.arange(fsdp) * tp_size + tp).astype(jnp.int32)
    picked = pick(hidden, norm_gain[None, :], blocks, fsdp, rows)
    x = lax.all_to_all(jnp.stack(picked), "fsdp", 0, 0, tiled=True)
    x = x.reshape(fsdp * tokens, rows)
    up2 = up * jnp.bfloat16(adapter_scale)
    cosine, sine_part = turn_tables(hidden, positions)
    out = None
    after = ()
    for chunk in range(chunks):
        owners = jnp.arange(tp_size, dtype=jnp.int32)[:, None] * (share // width)
        offsets = jnp.arange(steps, dtype=jnp.int32)[None, :] + chunk * steps
        _, *parts = quantize_and_project(
            base, down, up2, x, (owners + offsets).reshape(-1), tp_size * steps, width,
            groups=tp_size, after=after,
        )
        mine = lax.psum_scatter(jnp.stack(parts), "tp", scatter_dimension=0, tiled=True)[0]
        mine = lax.psum_scatter(mine, "fsdp", scatter_dimension=0, tiled=True)
        out = turn(cosine, sine_part, (mine,), chunk, chunks, out)
        after = (mine,)
    return out


def solution(mesh):
    fsdp, tp = mesh.shape["fsdp"], mesh.shape["tp"]
    if (fsdp, tp) == (4, 4):
        shards = line_shards
    else:
        shards = functools.partial(any_shards, fsdp, tp)
    placed = (
        P(("rep", "fsdp"), None),
        P(("rep", "fsdp", "tp"), None),
        P(("rep", "fsdp", "tp"), None),
        P("rep", None),
        P("rep"),
        P(("rep", "fsdp")),
    )
    return jax.shard_map(
        shards, mesh=mesh, in_specs=placed, out_specs=P(("rep", "fsdp"), "tp"), check_vma=False
    )
```

```python
import functools
import math

import jax
import jax.numpy as jnp
from jax import lax
from jax.experimental import pallas as pl
from jax.experimental.pallas import tpu as pltpu
from jax.sharding import PartitionSpec as P

HEAD = 128
BLOCK = 128
PIECES = 4
TILE = 512


norm_epsilon = 1e-05
scale_epsilon = 1e-06
code_limit = 15.0
adapter_scale = 2.0
rope_theta = 500000.0
rope_factor = 8.0
low_factor = 1.0
high_factor = 4.0
initial_context = 8192.0
feature_scale = 1024.0

ANY = pl.BlockSpec(memory_space=pl.ANY)


def params(mebibytes):
    return pltpu.CompilerParams(vmem_limit_bytes=mebibytes << 20)


def cost(flops, nbytes):
    return pl.CostEstimate(flops=int(flops), bytes_accessed=int(nbytes), transcendentals=0)


def like(shape, dtype=jnp.bfloat16):
    return jax.ShapeDtypeStruct(shape, dtype)


def frequencies(positions):
    pair_index = jnp.arange(HEAD // 2, dtype=jnp.float32)
    inverse = jnp.exp(pair_index * (-2.0 * math.log(rope_theta) / HEAD))
    wavelength = 2.0 * math.pi / inverse
    blend = (initial_context / wavelength - low_factor) / (high_factor - low_factor)
    middle = (1.0 - blend) * inverse / rope_factor + blend * inverse
    adjusted = jnp.where(
        wavelength < initial_context / high_factor,
        inverse,
        jnp.where(wavelength > initial_context / low_factor, inverse / rope_factor, middle),
    )
    angles = positions.astype(jnp.float32)[:, None] * adjusted[None, :]
    return (jnp.cos(angles), jnp.sin(angles))


def turn_tables(hidden, positions):
    values = hidden.astype(jnp.float32)
    mean_square = jnp.mean(values * values, axis=1, keepdims=True)
    factor = lax.rsqrt(mean_square + norm_epsilon) * (1.0 / feature_scale)
    cosine, sine_part = frequencies(positions)
    return (
        jnp.concatenate([cosine, cosine], axis=1) * factor,
        jnp.concatenate([-sine_part, sine_part], axis=1) * factor,
    )


def pick_kernel(table, *refs):
    count = len(refs) // 3
    for i in range(count):
        values, gain, out = refs[i], refs[count + i], refs[2 * count + i]
        scaled = values[...].astype(jnp.float32) * (gain[...].astype(jnp.float32) * feature_scale)
        out[...] = scaled.astype(jnp.bfloat16)


def pick(hidden, norm_gain, table, count, width):
    tokens = hidden.shape[0]

    def spec(rows, i):
        return pl.BlockSpec((rows, width), lambda step, table: (0, table[i]))

    return pl.pallas_call(
        pick_kernel,
        grid_spec=pltpu.PrefetchScalarGridSpec(
            num_scalar_prefetch=1,
            grid=(1,),
            in_specs=[spec(tokens, i) for i in range(count)] + [spec(1, i) for i in range(count)],
            out_specs=[pl.BlockSpec((tokens, width), lambda step, table: (0, 0))] * count,
        ),
        out_shape=[like((tokens, width))] * count,
        compiler_params=params(60),
        name="pick_features",
    )(table, *([hidden] * count), *([norm_gain] * count))


def scales_of(largest):
    ratio = (largest + scale_epsilon) / code_limit
    scale = jnp.exp2(jnp.ceil(jnp.log2(ratio))).astype(jnp.bfloat16).astype(jnp.float32)
    scale = jnp.where(ratio > scale, scale * 2.0, scale)
    return jnp.where(ratio <= scale * 0.5, scale * 0.5, scale)


def quantize_tile(base, down, up, weight, first, merged, scale_scratch):
    rows, width = base.shape
    row_blocks = rows // BLOCK
    first_block = first // BLOCK
    tops = []
    for i in range(row_blocks):
        block_rows = pl.ds(i * BLOCK, BLOCK)
        here = pl.ds(first + i * BLOCK, BLOCK)
        low_rank = jnp.dot(down[here, :], up[...], preferred_element_type=jnp.float32)
        total = base[block_rows, :].astype(jnp.float32) + low_rank
        merged[here, :] = total
        tops.append(jnp.max(jnp.abs(total), axis=0, keepdims=True))
    top = jnp.concatenate(tops, axis=0)
    blocks = pl.ds(first_block, row_blocks)
    for j in range(width // BLOCK):
        cols = slice(j * BLOCK, (j + 1) * BLOCK)
        largest = jnp.max(top[:, cols], axis=1, keepdims=True)
        scale = scales_of(jnp.broadcast_to(largest, (row_blocks, BLOCK)))
        scale_scratch[0, blocks, cols] = scale
        scale_scratch[1, blocks, cols] = 1.0 / scale
    for i in range(row_blocks):
        here = pl.ds(first + i * BLOCK, BLOCK)
        scale = scale_scratch[0, pl.ds(first_block + i, 1), :]
        inverse = scale_scratch[1, pl.ds(first_block + i, 1), :]
        codes = jnp.floor(merged[here, :] * inverse + 0.5)
        weight[here, :] = codes.astype(jnp.bfloat16) * scale.astype(jnp.bfloat16)


def gather_features(pieces, x):
    @pl.when(pl.program_id(0) == 0)
    def _():
        row = 0
        for line in pieces:
            col = 0
            for piece in line:
                x[row : row + piece.shape[0], col : col + piece.shape[1]] = piece[...]
                col += piece.shape[1]
            row += line[0].shape[0]


def store_rows(product, outs):
    first = 0
    for out in outs:
        out[...] = product[first : first + out.shape[0], :].astype(jnp.bfloat16)
        first += out.shape[0]


def split_lines(refs, shape):
    lines = []
    for length in shape:
        lines.append(refs[:length])
        refs = refs[length:]
    return lines, refs


def pass_kernel(sources, shape, late, after, keep, outs, carry, table, *refs):
    if carry:
        end = len(refs) - (3 if keep else 4)
        for k in range(carry):
            refs[end - carry + k][...] = refs[k][...]
        refs = refs[carry : end - carry] + refs[end:]
    bases, refs = refs[:sources], refs[sources:]
    (down, up), refs = refs[:2], refs[2:]
    kept, refs = (refs[0], refs[1:]) if late else (None, refs)
    lines, refs = split_lines(refs, shape)
    refs = refs[after:]
    place = 0 if keep else outs
    weight, refs = refs[place], refs[:place] + refs[place + 1 :]
    outs, (x, merged, scale_scratch) = refs[:outs], refs[outs:]
    if lines:
        gather_features(lines, x)
    products = []
    if late:
        tokens = lines[-1][0].shape[0]
        last = x[x.shape[0] - tokens :, :]
        products.append(jnp.dot(last, kept[...], preferred_element_type=jnp.float32))
    rows = bases[0].shape[0]
    for i, base in enumerate(bases):
        quantize_tile(base, down, up, weight, i * rows, merged, scale_scratch)
    if lines:
        products.append(jnp.dot(x[...], weight[...], preferred_element_type=jnp.float32))
        store_rows(jnp.concatenate(products, axis=0) if late else products[0], outs)


def row_outs(out_rows, steps, width):
    def spec(count, block):
        return pl.BlockSpec((count, width), lambda i, *_: (block, i))

    shapes = [like((total, steps * width)) for _, _, total in out_rows]
    return shapes, [spec(count, block) for count, block, _ in out_rows]


def merge_pass(
    bases, down, up, table, steps, width, lines=(), out_rows=(), kept=None, keep=False, carry=None,
    onto=None, after=(),
):
    rows = bases[0][0].shape[0]
    depth, rank = down.shape
    tokens = sum(line[0].shape[0] for line in lines)

    def fixed(shape):
        return pl.BlockSpec(shape, lambda i, table: (0, 0))

    def tile(height, place):
        if place is None:
            return pl.BlockSpec((height, width), lambda i, table: (0, table[i]))
        return pl.BlockSpec((height, width), lambda i, table: (0, place + i))

    operands = [base for base, _ in bases] + [down, up]
    in_specs = [tile(rows, place) for _, place in bases] + [fixed(down.shape), tile(rank, None)]
    if kept is not None:
        operands.append(kept)
        in_specs.append(tile(depth, 0))
    for line in lines:
        operands += line
        in_specs += [fixed(piece.shape) for piece in line]
    if onto is not None:
        after = (onto, *after)
    operands += after
    in_specs += [ANY] * len(after)
    out_shape, out_specs = row_outs(out_rows, steps, width)
    carried = 0
    if carry is not None:
        values, span, carried = carry
        block = (values.shape[0], span)

        def carry_spec(k):
            return pl.BlockSpec(block, lambda i, table: (0, table[steps + k * steps + i]))

        operands = [values] * carried + operands
        in_specs = [carry_spec(k) for k in range(carried)] + in_specs
    scratch = [
        pltpu.VMEM((max(tokens, 16), depth), jnp.bfloat16),
        pltpu.VMEM((depth, width), jnp.float32),
        pltpu.VMEM((2, depth // BLOCK, width), jnp.float32),
    ]
    if keep:
        out_shape.insert(0, like((depth, steps * width)))
        out_specs.insert(0, tile(depth, 0))
    else:
        scratch.insert(0, pltpu.VMEM((depth, width), jnp.bfloat16))
    if carry is not None:
        out_shape += [like((block[0], steps * span))] * carried
        out_specs += [pl.BlockSpec(block, lambda i, table: (0, i))] * carried
    return pl.pallas_call(
        functools.partial(
            pass_kernel, len(bases), [len(line) for line in lines], kept is not None, len(after),
            keep, len(out_rows), carried,
        ),
        grid_spec=pltpu.PrefetchScalarGridSpec(
            num_scalar_prefetch=1,
            grid=(steps,),
            in_specs=in_specs,
            out_specs=out_specs,
            scratch_shapes=scratch,
        ),
        out_shape=out_shape,
        input_output_aliases={} if onto is None else {1 + len(operands) - len(after): 0},
        cost_estimate=cost(2 * tokens * depth * steps * width, 4 * depth * steps * width),
        compiler_params=params(42 if carried else 28),
        name="merge_pass",
    )(table, *operands)


def project_kernel(shape, after, outs, weight, *refs):
    lines, refs = split_lines(refs, shape)
    outs, x = refs[after : after + outs], refs[-1]
    gather_features(lines, x)
    store_rows(jnp.dot(x[...], weight[...], preferred_element_type=jnp.float32), outs)


def project(weight, steps, lines, out_rows, after=()):
    depth, columns = weight.shape
    width = columns // steps
    tokens = sum(line[0].shape[0] for line in lines)
    pieces = [piece for line in lines for piece in line]
    out_shape, out_specs = row_outs(out_rows, steps, width)
    return pl.pallas_call(
        functools.partial(project_kernel, [len(line) for line in lines], len(after), len(out_rows)),
        grid=(steps,),
        in_specs=[pl.BlockSpec((depth, width), lambda i: (0, i))]
        + [pl.BlockSpec(piece.shape, lambda i: (0, 0)) for piece in pieces]
        + [ANY] * len(after),
        out_specs=out_specs,
        out_shape=out_shape,
        scratch_shapes=[pltpu.VMEM((tokens, depth), jnp.bfloat16)],
        cost_estimate=cost(2 * tokens * depth * columns, 2 * depth * columns),
        compiler_params=params(20),
        name="project",
    )(weight, *pieces, *after)


def take_kernel(table, values, *refs):
    refs[-1][...] = values[...]


def take_tiles(values, table, steps, width, after=()):
    rows = values.shape[0]
    return pl.pallas_call(
        take_kernel,
        grid_spec=pltpu.PrefetchScalarGridSpec(
            num_scalar_prefetch=1,
            grid=(steps,),
            in_specs=[pl.BlockSpec((rows, width), lambda i, table: (0, table[i]))]
            + [ANY] * len(after),
            out_specs=pl.BlockSpec((rows, width), lambda i, table: (0, i)),
        ),
        out_shape=like((rows, steps * width)),
        compiler_params=params(40),
        name="take_tiles",
    )(table, values, *after)


def turn_kernel(count, cosine, sine_part, *refs):
    out = refs[-1]
    for j in range(out.shape[1] // HEAD):
        cols = slice(j * HEAD, (j + 1) * HEAD)
        total = refs[0][:, cols].astype(jnp.float32)
        for term in refs[1:count]:
            total = total + term[:, cols].astype(jnp.float32)
        swapped = pltpu.roll(total, HEAD // 2, 1)
        turned = total * cosine[...] + swapped * sine_part[...]
        out[:, cols] = turned.astype(jnp.bfloat16)


def turn(cosine, sine_part, terms, place, places, into, after=()):
    tokens = cosine.shape[0]
    columns = terms[0][0].shape[1]
    width = math.gcd(columns, place) if place else columns
    table = pl.BlockSpec((tokens, HEAD), lambda i: (0, 0))

    def term_spec(block):
        return pl.BlockSpec((tokens, width), lambda i: (block, i))

    extra = [] if into is None else [into]
    count = len(terms)
    return pl.pallas_call(
        functools.partial(turn_kernel, count),
        grid=(columns // width,),
        in_specs=[table] * 2 + [term_spec(block) for _, block in terms]
        + [ANY] * (len(extra) + len(after)),
        out_specs=pl.BlockSpec((tokens, width), lambda i: (0, place // width + i)),
        out_shape=like((tokens, places)),
        input_output_aliases={2 + count: 0} if extra else {},
        compiler_params=params(12),
        name="turn",
    )(cosine, sine_part, *[term for term, _ in terms], *extra, *after)


def add_kernel(count, *refs):
    total = refs[0][...].astype(jnp.float32)
    for term in refs[1:count]:
        total = total + term[...].astype(jnp.float32)
    refs[-1][...] = total.astype(jnp.bfloat16)


def added(terms, rows, after=()):
    columns = terms[0][0].shape[1]
    width = tile_width(columns, 512)

    def term_spec(block):
        return pl.BlockSpec((rows, width), lambda i: (block, i))

    return pl.pallas_call(
        functools.partial(add_kernel, len(terms)),
        grid=(columns // width,),
        in_specs=[term_spec(block) for _, block in terms] + [ANY] * len(after),
        out_specs=term_spec(0),
        out_shape=like((rows, columns)),
        compiler_params=params(12),
        name="add_terms",
    )(*[term for term, _ in terms], *after)


def tile_width(columns, most):
    width = min(columns, most)
    while columns % width:
        width //= 2
    return width


def line_shards(hidden, base, down, up, norm_gain, positions):
    tp = lax.axis_index("tp")
    z = lax.axis_index("fsdp")
    rows, all_columns = base.shape
    tokens = hidden.shape[0]
    quarter = all_columns // 4
    other_core, other_chip, other_both = tp ^ 1, tp ^ 2, tp ^ 3

    def over(axis, distance):
        return functools.partial(
            lax.ppermute, axis_name=axis, perm=[(i, i ^ distance) for i in range(4)]
        )

    over_core, over_y = over("tp", 1), over("tp", 2)
    over_z1, over_z2 = over("fsdp", 1), over("fsdp", 2)

    piece = quarter // PIECES
    width = tile_width(piece, min(TILE, piece // 2))
    steps = piece // width

    def tiles(*places):
        offsets = jnp.arange(steps, dtype=jnp.int32)
        starts = [owner * (quarter // width) + i * steps for owner, i in places]
        return jnp.concatenate([start + offsets for start in starts]).astype(jnp.int32)

    blocks = [(z ^ d) * 4 + tp for d in range(4)] + [z * 4 + other_core]
    own_x, p1, p2, p3, own_other = pick(
        hidden, norm_gain[None, :], jnp.stack(blocks).astype(jnp.int32), 5, rows
    )
    x1, x2, x3 = over("fsdp", 1)(p1), over("fsdp", 2)(p2), over("fsdp", 3)(p3)
    first_lines = [[x1, over_core(x1)], [x3, over_core(x3)], [own_x, own_other]]
    all_lines = [*first_lines, [x2, over_core(x2)]]

    down2 = jnp.concatenate([down, over_core(down)], axis=0)
    up2 = up * jnp.bfloat16(adapter_scale)

    def spans(names, count):
        span = min(piece, piece * len(names) // count)
        each = piece // span
        owners = [(other_both if kind == "y" else other_core) for kind, _ in names]
        firsts = [(owner * PIECES + i) * each for owner, (_, i) in zip(owners, names)]
        blocks = [first + k for first in firsts for k in range(each)]
        return jnp.stack(blocks).astype(jnp.int32), span

    received = {}

    def send(taken, names):
        arrived = over_core(taken)
        for k, name in enumerate(names):
            received[name] = (arrived, k * steps)

    def take(names, after):
        table, span = spans(names, len(names))
        taken = take_tiles(base, table, len(names), span, after)
        send(taken, names)
        return taken

    taken = take([("y", 0)], (own_x,))
    taken = take([("y", 1), ("own", 0), ("y", 2)], (taken, down2))

    def run_pass(owner, i, kind, carried, **options):
        table = tiles((owner, i))
        carry = None
        if carried:
            blocks, span = spans(sum(carried, []), steps * len(carried))
            table = jnp.concatenate([table, blocks])
            carry = (base, span, len(carried))
        outs = merge_pass(
            [(base, None), received[kind, i]], down2, up2, table, steps, width, carry=carry, **options,
        )
        if carried:
            outs, taken = outs[: -len(carried)], outs[-len(carried) :]
            for value, names in zip(taken, carried):
                send(value, names)
        return outs

    first_rows = [(2 * tokens, 0, 2 * tokens), (tokens, 0, 2 * tokens)]
    second_rows = [(tokens, 1, 2 * tokens), (2 * tokens, 0, 2 * tokens)] + [(tokens, 0, tokens)] * 2
    weights, halves, far_y, mid_y = {}, {}, {}, {}
    near, own, far, near_z, far_z = {}, {}, {}, {}, {}

    def weigh(i, after, carried=()):
        (weights[i],) = run_pass(other_chip, i, "y", carried, keep=True, after=after)

    def send_first(i, outs):
        value, halves[i] = outs
        far_y[i] = over_y(value)
        return value

    def first(i, after):
        weights[i], *outs = run_pass(
            other_chip, i, "y", (), lines=first_lines, out_rows=first_rows, keep=True, after=after
        )
        return send_first(i, outs)

    def second(i, after):
        half, near[i], own[i], far[i] = run_pass(
            tp, i, "own", (), lines=all_lines, out_rows=second_rows, kept=weights[i],
            onto=halves[i], after=after,
        )
        mid_y[i] = over_y(half)
        return half

    def to_z1(i, after):
        operand = added([(near[i], 0), (far_y[i], 0)], 2 * tokens, after)
        near_z[i] = over_z1(operand)
        return operand

    def to_z2(i, after):
        operand = added([(far[i], 0), (mid_y[i], 1), (near_z[i], 1)], tokens, after)
        far_z[i] = over_z2(operand)
        return operand

    def finish(i, out, after):
        terms = [(own[i], 0), (mid_y[i], 0), (near_z[i], 0), (far_z[i], 0)]
        return turn(cosine, sine_part, terms, i * piece, quarter, out, after)

    early_xs = sum(first_lines, [])
    weigh(0, (taken, *early_xs), [[("own", 1), ("y", 3)], [("own", 2), ("own", 3)]])
    done = send_first(0, project(weights[0], steps, first_lines, first_rows))
    done = first(1, (done,))
    done = second(0, (done, received["own", 2][0]))
    done = to_z1(0, (done,))
    done = first(2, (done,))
    done = second(1, (done,))
    done = to_z1(1, (done,))
    done = to_z2(0, (done,))
    done = first(3, (done,))
    done = second(2, (done,))
    done = to_z1(2, (done,))
    cosine, sine_part = turn_tables(lax.optimization_barrier((hidden, done))[0], positions)
    out = finish(0, None, (done,))
    done = to_z2(1, (out,))
    done = second(3, (done,))
    done = to_z1(3, (done,))
    out = finish(1, out, (done,))
    done = to_z2(2, (out,))
    out = finish(2, out, (done,))
    done = to_z2(3, (out,))
    return finish(3, out, (done,))


def any_shards(fsdp, tp_size, hidden, base, down, up, norm_gain, positions):
    tp = lax.axis_index("tp")
    rows, all_columns = base.shape
    tokens = hidden.shape[0]
    share = all_columns // tp_size
    chunks = max(1, share // 256)
    piece = share // chunks
    width = tile_width(piece, TILE)
    steps = piece // width

    blocks = (jnp.arange(fsdp) * tp_size + tp).astype(jnp.int32)
    picked = pick(hidden, norm_gain[None, :], blocks, fsdp, rows)
    x = lax.all_to_all(jnp.stack(picked), "fsdp", 0, 0, tiled=True)
    x = x.reshape(fsdp * tokens, rows)
    up2 = up * jnp.bfloat16(adapter_scale)
    cosine, sine_part = turn_tables(hidden, positions)
    out = None
    after = ()
    for chunk in range(chunks):
        owners = jnp.arange(tp_size, dtype=jnp.int32)[:, None] * (share // width)
        offsets = jnp.arange(steps, dtype=jnp.int32)[None, :] + chunk * steps
        (products,) = merge_pass(
            [(base, None)], down, up2, (owners + offsets).reshape(-1), tp_size * steps, width,
            [[x]], [(fsdp * tokens, 0, fsdp * tokens)], after=after,
        )
        products = products.reshape(fsdp * tokens, tp_size, piece).swapaxes(0, 1)
        mine = lax.psum_scatter(products, "tp", scatter_dimension=0, tiled=True)[0]
        mine = lax.psum_scatter(mine, "fsdp", scatter_dimension=0, tiled=True)
        out = turn(cosine, sine_part, [(mine, 0)], chunk * piece, share, out)
        after = (mine,)
    return out


def solution(mesh):
    fsdp, tp = mesh.shape["fsdp"], mesh.shape["tp"]
    if (fsdp, tp) == (4, 4):
        shards = line_shards
    else:
        shards = functools.partial(any_shards, fsdp, tp)
    placed = (
        P(("rep", "fsdp"), None),
        P(("rep", "fsdp", "tp"), None),
        P(("rep", "fsdp", "tp"), None),
        P("rep", None),
        P("rep"),
        P(("rep", "fsdp")),
    )
    return jax.shard_map(
        shards, mesh=mesh, in_specs=placed, out_specs=P(("rep", "fsdp"), "tp"), check_vma=False
    )
```

```python
import functools
import math

import jax
import jax.numpy as jnp
from jax import lax
from jax.experimental import pallas as pl
from jax.experimental.pallas import tpu as pltpu
from jax.sharding import PartitionSpec as P

HEAD = 128
BLOCK = 128
PIECES = 4
TILE = 512


norm_epsilon = 1e-05
scale_epsilon = 1e-06
code_limit = 15.0
adapter_scale = 2.0
rope_theta = 500000.0
rope_factor = 8.0
low_factor = 1.0
high_factor = 4.0
initial_context = 8192.0
feature_scale = 1024.0

ANY = pl.BlockSpec(memory_space=pl.ANY)


def params(mebibytes):
    return pltpu.CompilerParams(vmem_limit_bytes=mebibytes << 20)


def cost(flops, nbytes):
    return pl.CostEstimate(flops=int(flops), bytes_accessed=int(nbytes), transcendentals=0)


def like(shape, dtype=jnp.bfloat16):
    return jax.ShapeDtypeStruct(shape, dtype)


def frequencies(positions):
    pair_index = jnp.arange(HEAD // 2, dtype=jnp.float32)
    inverse = jnp.exp(pair_index * (-2.0 * math.log(rope_theta) / HEAD))
    wavelength = 2.0 * math.pi / inverse
    blend = (initial_context / wavelength - low_factor) / (high_factor - low_factor)
    middle = (1.0 - blend) * inverse / rope_factor + blend * inverse
    adjusted = jnp.where(
        wavelength < initial_context / high_factor,
        inverse,
        jnp.where(wavelength > initial_context / low_factor, inverse / rope_factor, middle),
    )
    angles = positions.astype(jnp.float32)[:, None] * adjusted[None, :]
    return (jnp.cos(angles), jnp.sin(angles))


def turn_tables(hidden, positions):
    values = hidden.astype(jnp.float32)
    mean_square = jnp.mean(values * values, axis=1, keepdims=True)
    factor = lax.rsqrt(mean_square + norm_epsilon) * (1.0 / feature_scale)
    cosine, sine_part = frequencies(positions)
    return (
        jnp.concatenate([cosine, cosine], axis=1) * factor,
        jnp.concatenate([-sine_part, sine_part], axis=1) * factor,
    )


def pick_kernel(table, *refs):
    count = len(refs) // 3
    for i in range(count):
        values, gain, out = refs[i], refs[count + i], refs[2 * count + i]
        scaled = values[...].astype(jnp.float32) * (gain[...].astype(jnp.float32) * feature_scale)
        out[...] = scaled.astype(jnp.bfloat16)


def pick(hidden, norm_gain, table, count, width):
    tokens = hidden.shape[0]

    def spec(rows, i):
        return pl.BlockSpec((rows, width), lambda step, table: (0, table[i]))

    return pl.pallas_call(
        pick_kernel,
        grid_spec=pltpu.PrefetchScalarGridSpec(
            num_scalar_prefetch=1,
            grid=(1,),
            in_specs=[spec(tokens, i) for i in range(count)] + [spec(1, i) for i in range(count)],
            out_specs=[pl.BlockSpec((tokens, width), lambda step, table: (0, 0))] * count,
        ),
        out_shape=[like((tokens, width))] * count,
        compiler_params=params(12),
        name="pick_features",
    )(table, *([hidden] * count), *([norm_gain] * count))


def scales_of(largest):
    ratio = (largest + scale_epsilon) / code_limit
    scale = jnp.exp2(jnp.ceil(jnp.log2(ratio))).astype(jnp.bfloat16).astype(jnp.float32)
    scale = jnp.where(ratio > scale, scale * 2.0, scale)
    return jnp.where(ratio <= scale * 0.5, scale * 0.5, scale)


def quantize_tile(base, down, up, weight, first, merged, scale_scratch):
    rows, width = base.shape
    row_blocks = rows // BLOCK
    first_block = first // BLOCK
    tops = []
    for i in range(row_blocks):
        block_rows = pl.ds(i * BLOCK, BLOCK)
        here = pl.ds(first + i * BLOCK, BLOCK)
        low_rank = jnp.dot(down[here, :], up[...], preferred_element_type=jnp.float32)
        total = base[block_rows, :].astype(jnp.float32) + low_rank
        merged[here, :] = total
        tops.append(jnp.max(jnp.abs(total), axis=0, keepdims=True))
    top = jnp.concatenate(tops, axis=0)
    blocks = pl.ds(first_block, row_blocks)
    for j in range(width // BLOCK):
        cols = slice(j * BLOCK, (j + 1) * BLOCK)
        largest = jnp.max(top[:, cols], axis=1, keepdims=True)
        scale = scales_of(jnp.broadcast_to(largest, (row_blocks, BLOCK)))
        scale_scratch[0, blocks, cols] = scale
        scale_scratch[1, blocks, cols] = 1.0 / scale
    for i in range(row_blocks):
        here = pl.ds(first + i * BLOCK, BLOCK)
        scale = scale_scratch[0, pl.ds(first_block + i, 1), :]
        inverse = scale_scratch[1, pl.ds(first_block + i, 1), :]
        codes = jnp.floor(merged[here, :] * inverse + 0.5)
        weight[here, :] = codes.astype(jnp.bfloat16) * scale.astype(jnp.bfloat16)


def gather_features(pieces, x):
    @pl.when(pl.program_id(0) == 0)
    def _():
        row = 0
        for line in pieces:
            col = 0
            for piece in line:
                x[row : row + piece.shape[0], col : col + piece.shape[1]] = piece[...]
                col += piece.shape[1]
            row += line[0].shape[0]


def store_rows(product, outs):
    first = 0
    for out in outs:
        out[...] = product[first : first + out.shape[0], :].astype(jnp.bfloat16)
        first += out.shape[0]


def split_lines(refs, shape):
    lines = []
    for length in shape:
        lines.append(refs[:length])
        refs = refs[length:]
    return lines, refs


def pass_kernel(sources, shape, late, after, keep, outs, carry, table, *refs):
    if carry:
        end = len(refs) - (3 if keep else 4)
        for k in range(carry):
            refs[end - carry + k][...] = refs[k][...]
        refs = refs[carry : end - carry] + refs[end:]
    bases, refs = refs[:sources], refs[sources:]
    (down, up), refs = refs[:2], refs[2:]
    kept, refs = (refs[0], refs[1:]) if late else (None, refs)
    lines, refs = split_lines(refs, shape)
    refs = refs[after:]
    place = 0 if keep else outs
    weight, refs = refs[place], refs[:place] + refs[place + 1 :]
    outs, (x, merged, scale_scratch) = refs[:outs], refs[outs:]
    if lines:
        gather_features(lines, x)
    products = []
    if late:
        tokens = lines[-1][0].shape[0]
        last = x[x.shape[0] - tokens :, :]
        products.append(jnp.dot(last, kept[...], preferred_element_type=jnp.float32))
    rows = bases[0].shape[0]
    for i, base in enumerate(bases):
        quantize_tile(base, down, up, weight, i * rows, merged, scale_scratch)
    if lines:
        products.append(jnp.dot(x[...], weight[...], preferred_element_type=jnp.float32))
        store_rows(jnp.concatenate(products, axis=0) if late else products[0], outs)


def row_outs(out_rows, steps, width):
    def spec(count, block):
        return pl.BlockSpec((count, width), lambda i, *_: (block, i))

    shapes = [like((total, steps * width)) for _, _, total in out_rows]
    return shapes, [spec(count, block) for count, block, _ in out_rows]


def merge_pass(
    bases, down, up, table, steps, width, lines=(), out_rows=(), kept=None, keep=False, carry=None,
    onto=None, after=(),
):
    rows = bases[0][0].shape[0]
    depth, rank = down.shape
    tokens = sum(line[0].shape[0] for line in lines)

    def fixed(shape):
        return pl.BlockSpec(shape, lambda i, table: (0, 0))

    def tile(height, place):
        if place is None:
            return pl.BlockSpec((height, width), lambda i, table: (0, table[i]))
        return pl.BlockSpec((height, width), lambda i, table: (0, place + i))

    operands = [base for base, _ in bases] + [down, up]
    in_specs = [tile(rows, place) for _, place in bases] + [fixed(down.shape), tile(rank, None)]
    if kept is not None:
        operands.append(kept)
        in_specs.append(tile(depth, 0))
    for line in lines:
        operands += line
        in_specs += [fixed(piece.shape) for piece in line]
    if onto is not None:
        after = (onto, *after)
    operands += after
    in_specs += [ANY] * len(after)
    out_shape, out_specs = row_outs(out_rows, steps, width)
    carried = 0
    if carry is not None:
        values, span, carried = carry
        block = (values.shape[0], span)

        def carry_spec(k):
            return pl.BlockSpec(block, lambda i, table: (0, table[steps + k * steps + i]))

        operands = [values] * carried + operands
        in_specs = [carry_spec(k) for k in range(carried)] + in_specs
    scratch = [
        pltpu.VMEM((max(tokens, 16), depth), jnp.bfloat16),
        pltpu.VMEM((depth, width), jnp.float32),
        pltpu.VMEM((2, depth // BLOCK, width), jnp.float32),
    ]
    if keep:
        out_shape.insert(0, pltpu.HBM((depth, steps * width), jnp.bfloat16))
        out_specs.insert(0, tile(depth, 0))
    else:
        scratch.insert(0, pltpu.VMEM((depth, width), jnp.bfloat16))
    if carry is not None:
        out_shape += [pltpu.HBM((block[0], steps * span), jnp.bfloat16)] * carried
        out_specs += [pl.BlockSpec(block, lambda i, table: (0, i))] * carried
    return pl.pallas_call(
        functools.partial(
            pass_kernel, len(bases), [len(line) for line in lines], kept is not None, len(after),
            keep, len(out_rows), carried,
        ),
        grid_spec=pltpu.PrefetchScalarGridSpec(
            num_scalar_prefetch=1,
            grid=(steps,),
            in_specs=in_specs,
            out_specs=out_specs,
            scratch_shapes=scratch,
        ),
        out_shape=out_shape,
        input_output_aliases={} if onto is None else {1 + len(operands) - len(after): 0},
        cost_estimate=cost(2 * tokens * depth * steps * width, 4 * depth * steps * width),
        compiler_params=params(42 if carried else 28),
        name="merge_pass",
    )(table, *operands)


def take_kernel(table, values, *refs):
    refs[-1][...] = values[...]


def take_tiles(values, table, steps, width, after=()):
    rows = values.shape[0]
    return pl.pallas_call(
        take_kernel,
        grid_spec=pltpu.PrefetchScalarGridSpec(
            num_scalar_prefetch=1,
            grid=(steps,),
            in_specs=[pl.BlockSpec((rows, width), lambda i, table: (0, table[i]))]
            + [ANY] * len(after),
            out_specs=pl.BlockSpec((rows, width), lambda i, table: (0, i)),
        ),
        out_shape=pltpu.HBM((rows, steps * width), jnp.bfloat16),
        compiler_params=params(40),
        name="take_tiles",
    )(table, values, *after)


def turn_kernel(count, cosine, sine_part, *refs):
    out = refs[-1]
    for j in range(out.shape[1] // HEAD):
        cols = slice(j * HEAD, (j + 1) * HEAD)
        total = refs[0][:, cols].astype(jnp.float32)
        for term in refs[1:count]:
            total = total + term[:, cols].astype(jnp.float32)
        swapped = pltpu.roll(total, HEAD // 2, 1)
        turned = total * cosine[...] + swapped * sine_part[...]
        out[:, cols] = turned.astype(jnp.bfloat16)


def turn(cosine, sine_part, terms, place, places, into, after=()):
    tokens = cosine.shape[0]
    columns = terms[0][0].shape[1]
    width = math.gcd(columns, place) if place else columns
    table = pl.BlockSpec((tokens, HEAD), lambda i: (0, 0))

    def term_spec(block):
        return pl.BlockSpec((tokens, width), lambda i: (block, i))

    extra = [] if into is None else [into]
    count = len(terms)
    return pl.pallas_call(
        functools.partial(turn_kernel, count),
        grid=(columns // width,),
        in_specs=[table] * 2 + [term_spec(block) for _, block in terms]
        + [ANY] * (len(extra) + len(after)),
        out_specs=pl.BlockSpec((tokens, width), lambda i: (0, place // width + i)),
        out_shape=like((tokens, places)),
        input_output_aliases={2 + count: 0} if extra else {},
        compiler_params=params(12),
        name="turn",
    )(cosine, sine_part, *[term for term, _ in terms], *extra, *after)


def add_kernel(count, *refs):
    total = refs[0][...].astype(jnp.float32)
    for term in refs[1:count]:
        total = total + term[...].astype(jnp.float32)
    refs[-1][...] = total.astype(jnp.bfloat16)


def added(terms, rows, after=()):
    columns = terms[0][0].shape[1]
    width = tile_width(columns, 512)

    def term_spec(block):
        return pl.BlockSpec((rows, width), lambda i: (block, i))

    return pl.pallas_call(
        functools.partial(add_kernel, len(terms)),
        grid=(columns // width,),
        in_specs=[term_spec(block) for _, block in terms] + [ANY] * len(after),
        out_specs=term_spec(0),
        out_shape=like((rows, columns)),
        compiler_params=params(12),
        name="add_terms",
    )(*[term for term, _ in terms], *after)


def tile_width(columns, most):
    width = min(columns, most)
    while columns % width:
        width //= 2
    return width


def line_shards(hidden, base, down, up, norm_gain, positions):
    tp = lax.axis_index("tp")
    z = lax.axis_index("fsdp")
    rows, all_columns = base.shape
    tokens = hidden.shape[0]
    quarter = all_columns // 4
    other_core, other_chip, other_both = tp ^ 1, tp ^ 2, tp ^ 3

    def over(axis, distance):
        return functools.partial(
            lax.ppermute, axis_name=axis, perm=[(i, i ^ distance) for i in range(4)]
        )

    over_core, over_y = over("tp", 1), over("tp", 2)
    over_z1, over_z2 = over("fsdp", 1), over("fsdp", 2)

    piece = quarter // PIECES
    width = tile_width(piece, min(TILE, piece // 2))
    steps = piece // width

    def tiles(*places):
        offsets = jnp.arange(steps, dtype=jnp.int32)
        starts = [owner * (quarter // width) + i * steps for owner, i in places]
        return jnp.concatenate([start + offsets for start in starts]).astype(jnp.int32)

    blocks = [(z ^ d) * 4 + tp for d in range(4)] + [z * 4 + other_core]
    own_x, p1, p2, p3, own_other = pick(
        hidden, norm_gain[None, :], jnp.stack(blocks).astype(jnp.int32), 5, rows
    )
    x1, x2, x3 = over("fsdp", 1)(p1), over("fsdp", 2)(p2), over("fsdp", 3)(p3)
    first_lines = [[x1, over_core(x1)], [x3, over_core(x3)], [own_x, own_other]]

    down2 = jnp.concatenate([down, over_core(down)], axis=0)
    up2 = up * jnp.bfloat16(adapter_scale)

    def spans(names, count):
        span = min(piece, piece * len(names) // count)
        each = piece // span
        owners = [(other_both if kind == "y" else other_core) for kind, _ in names]
        firsts = [(owner * PIECES + i) * each for owner, (_, i) in zip(owners, names)]
        blocks = [first + k for first in firsts for k in range(each)]
        return jnp.stack(blocks).astype(jnp.int32), span

    received = {}

    def send(taken, names):
        arrived = over_core(taken)
        for k, name in enumerate(names):
            received[name] = (arrived, k * steps)

    def take(names, after):
        table, span = spans(names, len(names))
        taken = take_tiles(base, table, len(names), span, after)
        send(taken, names)
        return taken

    taken = take([("y", 0)], (own_x,))
    taken = take([("y", 1), ("own", 0), ("y", 2)], (taken, down2))

    def run_pass(owner, i, kind, carried, **options):
        table = tiles((owner, i))
        carry = None
        if carried:
            blocks, span = spans(sum(carried, []), steps * len(carried))
            table = jnp.concatenate([table, blocks])
            carry = (base, span, len(carried))
        outs = merge_pass(
            [(base, None), received[kind, i]], down2, up2, table, steps, width, carry=carry, **options,
        )
        if carried:
            outs, taken = outs[: -len(carried)], outs[-len(carried) :]
            for value, names in zip(taken, carried):
                send(value, names)
        return outs

    first_rows = [(2 * tokens, 0, 2 * tokens), (tokens, 0, 2 * tokens)]
    second_rows = [(tokens, 1, 2 * tokens), (2 * tokens, 0, 2 * tokens)] + [(tokens, 0, tokens)] * 2
    weights, halves, far_y, mid_y = {}, {}, {}, {}
    near, own, far, near_z, far_z = {}, {}, {}, {}, {}

    def first(i, after, carried=()):
        weights[i], value, halves[i] = run_pass(
            other_chip, i, "y", carried, lines=first_lines, out_rows=first_rows, keep=True, after=after
        )
        far_y[i] = over_y(value)
        return value

    def second(i, after):
        half, near[i], own[i], far[i] = run_pass(
            tp, i, "own", (), lines=all_lines, out_rows=second_rows, kept=weights[i],
            onto=halves[i], after=after,
        )
        mid_y[i] = over_y(half)
        return half

    def to_z1(i, after):
        operand = added([(near[i], 0), (far_y[i], 0)], 2 * tokens, after)
        near_z[i] = over_z1(operand)
        return operand

    def to_z2(i, after):
        operand = added([(far[i], 0), (mid_y[i], 1), (near_z[i], 1)], tokens, after)
        far_z[i] = over_z2(operand)
        return operand

    def finish(i, out, after):
        terms = [(own[i], 0), (mid_y[i], 0), (near_z[i], 0), (far_z[i], 0)]
        return turn(cosine, sine_part, terms, i * piece, quarter, out, after)

    done = first(0, (taken,), [[("own", 1), ("y", 3)], [("own", 2), ("own", 3)]])
    k1 = first(1, (done,))
    done = first(2, (k1,))
    all_lines = [*first_lines, [x2, over_core(lax.optimization_barrier((x2, k1))[0])]]
    done = second(0, (done, received["own", 1][0], received["own", 2][0], far_y[0]))
    done = to_z1(0, (done,))
    done = second(1, (done, far_y[1]))
    done = to_z1(1, (done,))
    done = first(3, (done, far_y[2]))
    done = to_z2(0, (done,))
    done = second(2, (done,))
    cosine, sine_part = turn_tables(lax.optimization_barrier((hidden, done))[0], positions)
    out = finish(0, None, (done,))
    done = to_z2(1, (out,))
    done = to_z1(2, (done,))
    done = second(3, (done, far_y[3]))
    done = to_z1(3, (done,))
    out = finish(1, out, (done,))
    done = to_z2(2, (out,))
    done = to_z2(3, (done,))
    out = finish(2, out, (done,))
    return finish(3, out, (done,))


def any_shards(fsdp, tp_size, hidden, base, down, up, norm_gain, positions):
    tp = lax.axis_index("tp")
    rows, all_columns = base.shape
    tokens = hidden.shape[0]
    share = all_columns // tp_size
    chunks = max(1, share // 256)
    piece = share // chunks
    width = tile_width(piece, TILE)
    steps = piece // width

    blocks = (jnp.arange(fsdp) * tp_size + tp).astype(jnp.int32)
    picked = pick(hidden, norm_gain[None, :], blocks, fsdp, rows)
    x = lax.all_to_all(jnp.stack(picked), "fsdp", 0, 0, tiled=True)
    x = x.reshape(fsdp * tokens, rows)
    up2 = up * jnp.bfloat16(adapter_scale)
    cosine, sine_part = turn_tables(hidden, positions)
    out = None
    after = ()
    for chunk in range(chunks):
        owners = jnp.arange(tp_size, dtype=jnp.int32)[:, None] * (share // width)
        offsets = jnp.arange(steps, dtype=jnp.int32)[None, :] + chunk * steps
        (products,) = merge_pass(
            [(base, None)], down, up2, (owners + offsets).reshape(-1), tp_size * steps, width,
            [[x]], [(fsdp * tokens, 0, fsdp * tokens)], after=after,
        )
        products = products.reshape(fsdp * tokens, tp_size, piece).swapaxes(0, 1)
        mine = lax.psum_scatter(products, "tp", scatter_dimension=0, tiled=True)[0]
        mine = lax.psum_scatter(mine, "fsdp", scatter_dimension=0, tiled=True)
        out = turn(cosine, sine_part, [(mine, 0)], chunk * piece, share, out)
        after = (mine,)
    return out


def solution(mesh):
    fsdp, tp = mesh.shape["fsdp"], mesh.shape["tp"]
    if (fsdp, tp) == (4, 4):
        shards = line_shards
    else:
        shards = functools.partial(any_shards, fsdp, tp)
    placed = (
        P(("rep", "fsdp"), None),
        P(("rep", "fsdp", "tp"), None),
        P(("rep", "fsdp", "tp"), None),
        P("rep", None),
        P("rep"),
        P(("rep", "fsdp")),
    )
    return jax.shard_map(
        shards, mesh=mesh, in_specs=placed, out_specs=P(("rep", "fsdp"), "tp"), check_vma=False
    )
```

```python
import functools
import math

import jax
import jax.numpy as jnp
from jax import lax
from jax.experimental import pallas as pl
from jax.experimental.pallas import tpu as pltpu
from jax.sharding import PartitionSpec as P

HEAD = 128
BLOCK = 128
PIECES = 4
TILE = 512


norm_epsilon = 1e-05
scale_epsilon = 1e-06
code_limit = 15.0
adapter_scale = 2.0
rope_theta = 500000.0
rope_factor = 8.0
low_factor = 1.0
high_factor = 4.0
initial_context = 8192.0
feature_scale = 1024.0

ANY = pl.BlockSpec(memory_space=pl.ANY)


def params(mebibytes):
    return pltpu.CompilerParams(vmem_limit_bytes=mebibytes << 20)


def cost(flops, nbytes):
    return pl.CostEstimate(flops=int(flops), bytes_accessed=int(nbytes), transcendentals=0)


def like(shape, dtype=jnp.bfloat16):
    return jax.ShapeDtypeStruct(shape, dtype)


def frequencies(positions):
    pair_index = jnp.arange(HEAD // 2, dtype=jnp.float32)
    inverse = jnp.exp(pair_index * (-2.0 * math.log(rope_theta) / HEAD))
    wavelength = 2.0 * math.pi / inverse
    blend = (initial_context / wavelength - low_factor) / (high_factor - low_factor)
    middle = (1.0 - blend) * inverse / rope_factor + blend * inverse
    adjusted = jnp.where(
        wavelength < initial_context / high_factor,
        inverse,
        jnp.where(wavelength > initial_context / low_factor, inverse / rope_factor, middle),
    )
    angles = positions.astype(jnp.float32)[:, None] * adjusted[None, :]
    return (jnp.cos(angles), jnp.sin(angles))


def turn_tables(hidden, positions):
    values = hidden.astype(jnp.float32)
    mean_square = jnp.mean(values * values, axis=1, keepdims=True)
    factor = lax.rsqrt(mean_square + norm_epsilon) * (1.0 / feature_scale)
    cosine, sine_part = frequencies(positions)
    return (
        jnp.concatenate([cosine, cosine], axis=1) * factor,
        jnp.concatenate([-sine_part, sine_part], axis=1) * factor,
    )


def pick_kernel(table, *refs):
    count = len(refs) // 3
    for i in range(count):
        values, gain, out = refs[i], refs[count + i], refs[2 * count + i]
        scaled = values[...].astype(jnp.float32) * (gain[...].astype(jnp.float32) * feature_scale)
        out[...] = scaled.astype(jnp.bfloat16)


def pick(hidden, norm_gain, table, count, width):
    tokens = hidden.shape[0]

    def spec(rows, i):
        return pl.BlockSpec((rows, width), lambda step, table: (0, table[i]))

    return pl.pallas_call(
        pick_kernel,
        grid_spec=pltpu.PrefetchScalarGridSpec(
            num_scalar_prefetch=1,
            grid=(1,),
            in_specs=[spec(tokens, i) for i in range(count)] + [spec(1, i) for i in range(count)],
            out_specs=[pl.BlockSpec((tokens, width), lambda step, table: (0, 0))] * count,
        ),
        out_shape=[like((tokens, width))] * count,
        compiler_params=params(12),
        name="pick_features",
    )(table, *([hidden] * count), *([norm_gain] * count))


def scales_of(largest):
    ratio = (largest + scale_epsilon) / code_limit
    scale = jnp.exp2(jnp.ceil(jnp.log2(ratio))).astype(jnp.bfloat16).astype(jnp.float32)
    scale = jnp.where(ratio > scale, scale * 2.0, scale)
    return jnp.where(ratio <= scale * 0.5, scale * 0.5, scale)


def quantize_tile(base, down, up, weight, first, merged, scale_scratch):
    rows, width = base.shape
    row_blocks = rows // BLOCK
    first_block = first // BLOCK
    tops = []
    for i in range(row_blocks):
        block_rows = pl.ds(i * BLOCK, BLOCK)
        here = pl.ds(first + i * BLOCK, BLOCK)
        low_rank = jnp.dot(down[here, :], up[...], preferred_element_type=jnp.float32)
        total = base[block_rows, :].astype(jnp.float32) + low_rank
        merged[here, :] = total
        tops.append(jnp.max(jnp.abs(total), axis=0, keepdims=True))
    top = jnp.concatenate(tops, axis=0)
    blocks = pl.ds(first_block, row_blocks)
    for j in range(width // BLOCK):
        cols = slice(j * BLOCK, (j + 1) * BLOCK)
        largest = jnp.max(top[:, cols], axis=1, keepdims=True)
        scale = scales_of(jnp.broadcast_to(largest, (row_blocks, BLOCK)))
        scale_scratch[0, blocks, cols] = scale
        scale_scratch[1, blocks, cols] = 1.0 / scale
    for i in range(row_blocks):
        here = pl.ds(first + i * BLOCK, BLOCK)
        scale = scale_scratch[0, pl.ds(first_block + i, 1), :]
        inverse = scale_scratch[1, pl.ds(first_block + i, 1), :]
        codes = jnp.floor(merged[here, :] * inverse + 0.5)
        weight[here, :] = codes.astype(jnp.bfloat16) * scale.astype(jnp.bfloat16)


def gather_features(pieces, x):
    @pl.when(pl.program_id(0) == 0)
    def _():
        row = 0
        for line in pieces:
            col = 0
            for piece in line:
                x[row : row + piece.shape[0], col : col + piece.shape[1]] = piece[...]
                col += piece.shape[1]
            row += line[0].shape[0]


def store_rows(product, outs):
    first = 0
    for out in outs:
        out[...] = product[first : first + out.shape[0], :].astype(jnp.bfloat16)
        first += out.shape[0]


def split_lines(refs, shape):
    lines = []
    for length in shape:
        lines.append(refs[:length])
        refs = refs[length:]
    return lines, refs


def pass_kernel(sources, shape, late, after, keep, outs, carry, table, *refs):
    if carry:
        end = len(refs) - (3 if keep else 4)
        for k in range(carry):
            refs[end - carry + k][...] = refs[k][...]
        refs = refs[carry : end - carry] + refs[end:]
    bases, refs = refs[:sources], refs[sources:]
    (down, up), refs = refs[:2], refs[2:]
    kept, refs = (refs[0], refs[1:]) if late else (None, refs)
    lines, refs = split_lines(refs, shape)
    refs = refs[after:]
    place = 0 if keep else outs
    weight, refs = refs[place], refs[:place] + refs[place + 1 :]
    outs, (x, merged, scale_scratch) = refs[:outs], refs[outs:]
    if lines:
        gather_features(lines, x)
    products = []
    if late:
        tokens = lines[-1][0].shape[0]
        last = x[x.shape[0] - tokens :, :]
        products.append(jnp.dot(last, kept[...], preferred_element_type=jnp.float32))
    rows = bases[0].shape[0]
    for i, base in enumerate(bases):
        quantize_tile(base, down, up, weight, i * rows, merged, scale_scratch)
    if lines:
        products.append(jnp.dot(x[...], weight[...], preferred_element_type=jnp.float32))
        store_rows(jnp.concatenate(products, axis=0) if late else products[0], outs)


def row_outs(out_rows, steps, width):
    def spec(count, block):
        return pl.BlockSpec((count, width), lambda i, *_: (block, i))

    shapes = [like((total, steps * width)) for _, _, total in out_rows]
    return shapes, [spec(count, block) for count, block, _ in out_rows]


def merge_pass(
    bases, down, up, table, steps, width, lines=(), out_rows=(), kept=None, keep=False, carry=None,
    onto=None, after=(),
):
    rows = bases[0][0].shape[0]
    depth, rank = down.shape
    tokens = sum(line[0].shape[0] for line in lines)

    def fixed(shape):
        return pl.BlockSpec(shape, lambda i, table: (0, 0))

    def tile(height, place):
        if place is None:
            return pl.BlockSpec((height, width), lambda i, table: (0, table[i]))
        return pl.BlockSpec((height, width), lambda i, table: (0, place + i))

    operands = [base for base, _ in bases] + [down, up]
    in_specs = [tile(rows, place) for _, place in bases] + [fixed(down.shape), tile(rank, None)]
    if kept is not None:
        operands.append(kept)
        in_specs.append(tile(depth, 0))
    for line in lines:
        operands += line
        in_specs += [fixed(piece.shape) for piece in line]
    if onto is not None:
        after = (onto, *after)
    operands += after
    in_specs += [ANY] * len(after)
    out_shape, out_specs = row_outs(out_rows, steps, width)
    carried = 0
    if carry is not None:
        values, span, carried = carry
        block = (values.shape[0], span)

        def carry_spec(k):
            return pl.BlockSpec(block, lambda i, table: (0, table[steps + k * steps + i]))

        operands = [values] * carried + operands
        in_specs = [carry_spec(k) for k in range(carried)] + in_specs
    scratch = [
        pltpu.VMEM((max(tokens, 16), depth), jnp.bfloat16),
        pltpu.VMEM((depth, width), jnp.float32),
        pltpu.VMEM((2, depth // BLOCK, width), jnp.float32),
    ]
    if keep:
        out_shape.insert(0, pltpu.HBM((depth, steps * width), jnp.bfloat16))
        out_specs.insert(0, tile(depth, 0))
    else:
        scratch.insert(0, pltpu.VMEM((depth, width), jnp.bfloat16))
    if carry is not None:
        out_shape += [pltpu.HBM((block[0], steps * span), jnp.bfloat16)] * carried
        out_specs += [pl.BlockSpec(block, lambda i, table: (0, i))] * carried
    return pl.pallas_call(
        functools.partial(
            pass_kernel, len(bases), [len(line) for line in lines], kept is not None, len(after),
            keep, len(out_rows), carried,
        ),
        grid_spec=pltpu.PrefetchScalarGridSpec(
            num_scalar_prefetch=1,
            grid=(steps,),
            in_specs=in_specs,
            out_specs=out_specs,
            scratch_shapes=scratch,
        ),
        out_shape=out_shape,
        input_output_aliases={} if onto is None else {1 + len(operands) - len(after): 0},
        cost_estimate=cost(2 * tokens * depth * steps * width, 4 * depth * steps * width),
        compiler_params=params(42 if carried else 28),
        name="merge_pass",
    )(table, *operands)


def take_kernel(table, values, *refs):
    refs[-1][...] = values[...]


def take_tiles(values, table, steps, width, after=()):
    rows = values.shape[0]
    return pl.pallas_call(
        take_kernel,
        grid_spec=pltpu.PrefetchScalarGridSpec(
            num_scalar_prefetch=1,
            grid=(steps,),
            in_specs=[pl.BlockSpec((rows, width), lambda i, table: (0, table[i]))]
            + [ANY] * len(after),
            out_specs=pl.BlockSpec((rows, width), lambda i, table: (0, i)),
        ),
        out_shape=pltpu.HBM((rows, steps * width), jnp.bfloat16),
        compiler_params=params(40),
        name="take_tiles",
    )(table, values, *after)


def turn_kernel(count, cosine, sine_part, *refs):
    out = refs[-1]
    for j in range(out.shape[1] // HEAD):
        cols = slice(j * HEAD, (j + 1) * HEAD)
        total = refs[0][:, cols].astype(jnp.float32)
        for term in refs[1:count]:
            total = total + term[:, cols].astype(jnp.float32)
        swapped = pltpu.roll(total, HEAD // 2, 1)
        turned = total * cosine[...] + swapped * sine_part[...]
        out[:, cols] = turned.astype(jnp.bfloat16)


def turn(cosine, sine_part, terms, place, places, into, after=()):
    tokens = cosine.shape[0]
    columns = terms[0][0].shape[1]
    width = math.gcd(columns, place) if place else columns
    table = pl.BlockSpec((tokens, HEAD), lambda i: (0, 0))

    def term_spec(block):
        return pl.BlockSpec((tokens, width), lambda i: (block, i))

    extra = [] if into is None else [into]
    count = len(terms)
    return pl.pallas_call(
        functools.partial(turn_kernel, count),
        grid=(columns // width,),
        in_specs=[table] * 2 + [term_spec(block) for _, block in terms]
        + [ANY] * (len(extra) + len(after)),
        out_specs=pl.BlockSpec((tokens, width), lambda i: (0, place // width + i)),
        out_shape=like((tokens, places)),
        input_output_aliases={2 + count: 0} if extra else {},
        compiler_params=params(12),
        name="turn",
    )(cosine, sine_part, *[term for term, _ in terms], *extra, *after)


def add_kernel(count, *refs):
    total = refs[0][...].astype(jnp.float32)
    for term in refs[1:count]:
        total = total + term[...].astype(jnp.float32)
    refs[-1][...] = total.astype(jnp.bfloat16)


def added(terms, rows, after=()):
    columns = terms[0][0].shape[1]
    width = tile_width(columns, 512)

    def term_spec(block):
        return pl.BlockSpec((rows, width), lambda i: (block, i))

    return pl.pallas_call(
        functools.partial(add_kernel, len(terms)),
        grid=(columns // width,),
        in_specs=[term_spec(block) for _, block in terms] + [ANY] * len(after),
        out_specs=term_spec(0),
        out_shape=like((rows, columns)),
        compiler_params=params(12),
        name="add_terms",
    )(*[term for term, _ in terms], *after)


def tile_width(columns, most):
    width = min(columns, most)
    while columns % width:
        width //= 2
    return width


def line_shards(hidden, base, down, up, norm_gain, positions):
    tp = lax.axis_index("tp")
    z = lax.axis_index("fsdp")
    rows, all_columns = base.shape
    tokens = hidden.shape[0]
    quarter = all_columns // 4
    other_core, other_chip, other_both = tp ^ 1, tp ^ 2, tp ^ 3

    def over(axis, distance):
        return functools.partial(
            lax.ppermute, axis_name=axis, perm=[(i, i ^ distance) for i in range(4)]
        )

    over_core, over_y = over("tp", 1), over("tp", 2)
    over_z1, over_z2 = over("fsdp", 1), over("fsdp", 2)

    piece = quarter // PIECES
    width = tile_width(piece, min(TILE, piece // 2))
    steps = piece // width

    def tiles(*places):
        offsets = jnp.arange(steps, dtype=jnp.int32)
        starts = [owner * (quarter // width) + i * steps for owner, i in places]
        return jnp.concatenate([start + offsets for start in starts]).astype(jnp.int32)

    blocks = [(z ^ d) * 4 + tp for d in range(4)] + [z * 4 + other_core]
    own_x, p1, p2, p3, own_other = pick(
        hidden, norm_gain[None, :], jnp.stack(blocks).astype(jnp.int32), 5, rows
    )
    x1, x2, x3 = over("fsdp", 1)(p1), over("fsdp", 2)(p2), over("fsdp", 3)(p3)
    first_lines = [[x1, over_core(x1)], [x3, over_core(x3)], [own_x, own_other]]

    down2 = jnp.concatenate([down, over_core(down)], axis=0)
    up2 = up * jnp.bfloat16(adapter_scale)

    def spans(names, count):
        span = min(piece, piece * len(names) // count)
        each = piece // span
        owners = [(other_both if kind == "y" else other_core) for kind, _ in names]
        firsts = [(owner * PIECES + i) * each for owner, (_, i) in zip(owners, names)]
        blocks = [first + k for first in firsts for k in range(each)]
        return jnp.stack(blocks).astype(jnp.int32), span

    received = {}

    def send(taken, names):
        arrived = over_core(taken)
        for k, name in enumerate(names):
            received[name] = (arrived, k * steps)

    def take(names, after):
        table, span = spans(names, len(names))
        taken = take_tiles(base, table, len(names), span, after)
        send(taken, names)
        return taken

    taken = take([("y", 0)], (own_x,))
    taken = take([("y", 1), ("own", 0), ("y", 2)], (taken, down2))

    def run_pass(owner, i, kind, carried, **options):
        table = tiles((owner, i))
        carry = None
        if carried:
            blocks, span = spans(sum(carried, []), steps * len(carried))
            table = jnp.concatenate([table, blocks])
            carry = (base, span, len(carried))
        outs = merge_pass(
            [(base, None), received[kind, i]], down2, up2, table, steps, width, carry=carry, **options,
        )
        if carried:
            outs, taken = outs[: -len(carried)], outs[-len(carried) :]
            for value, names in zip(taken, carried):
                send(value, names)
        return outs

    first_rows = [(2 * tokens, 0, 2 * tokens), (tokens, 0, 2 * tokens)]
    second_rows = [(tokens, 1, 2 * tokens), (2 * tokens, 0, 2 * tokens)] + [(tokens, 0, tokens)] * 2
    weights, halves, far_y, mid_y = {}, {}, {}, {}
    near, own, far, near_z, far_z = {}, {}, {}, {}, {}

    def first(i, after, carried=()):
        weights[i], value, halves[i] = run_pass(
            other_chip, i, "y", carried, lines=first_lines, out_rows=first_rows, keep=True, after=after
        )
        far_y[i] = over_y(value)
        return value

    def second(i, after):
        half, near[i], own[i], far[i] = run_pass(
            tp, i, "own", (), lines=all_lines, out_rows=second_rows, kept=weights[i],
            onto=halves[i], after=after,
        )
        mid_y[i] = over_y(half)
        return half

    def to_z1(i, after):
        operand = added([(near[i], 0), (far_y[i], 0)], 2 * tokens, after)
        near_z[i] = over_z1(operand)
        return operand

    def to_z2(i, after):
        operand = added([(far[i], 0), (mid_y[i], 1), (near_z[i], 1)], tokens, after)
        far_z[i] = over_z2(operand)
        return operand

    def finish(i, out, after):
        terms = [(own[i], 0), (mid_y[i], 0), (near_z[i], 0), (far_z[i], 0)]
        return turn(cosine, sine_part, terms, i * piece, quarter, out, after)

    done = first(0, (taken,), [[("own", 1), ("y", 3)], [("own", 2), ("own", 3)]])
    k1 = first(1, (done,))
    done = first(2, (k1,))
    all_lines = [*first_lines, [x2, over_core(lax.optimization_barrier((x2, k1))[0])]]
    done = second(0, (done, received["own", 1][0], received["own", 2][0], far_y[0]))
    done = to_z1(0, (done,))
    done = second(1, (done, far_y[1]))
    done = to_z1(1, (done,))
    done = first(3, (done, far_y[2]))
    done = to_z2(0, (done,))
    done = second(2, (done,))
    done = to_z1(2, (done,))
    cosine, sine_part = turn_tables(lax.optimization_barrier((hidden, done))[0], positions)
    out = finish(0, None, (done,))
    done = to_z2(1, (out,))
    done = second(3, (done, far_y[3]))
    out = finish(1, out, (done,))
    done = to_z1(3, (out,))
    done = to_z2(2, (done,))
    done = to_z2(3, (done,))
    out = finish(2, out, (done,))
    return finish(3, out, ())


def any_shards(fsdp, tp_size, hidden, base, down, up, norm_gain, positions):
    tp = lax.axis_index("tp")
    rows, all_columns = base.shape
    tokens = hidden.shape[0]
    share = all_columns // tp_size
    chunks = max(1, share // 256)
    piece = share // chunks
    width = tile_width(piece, TILE)
    steps = piece // width

    blocks = (jnp.arange(fsdp) * tp_size + tp).astype(jnp.int32)
    picked = pick(hidden, norm_gain[None, :], blocks, fsdp, rows)
    x = lax.all_to_all(jnp.stack(picked), "fsdp", 0, 0, tiled=True)
    x = x.reshape(fsdp * tokens, rows)
    up2 = up * jnp.bfloat16(adapter_scale)
    cosine, sine_part = turn_tables(hidden, positions)
    out = None
    after = ()
    for chunk in range(chunks):
        owners = jnp.arange(tp_size, dtype=jnp.int32)[:, None] * (share // width)
        offsets = jnp.arange(steps, dtype=jnp.int32)[None, :] + chunk * steps
        (products,) = merge_pass(
            [(base, None)], down, up2, (owners + offsets).reshape(-1), tp_size * steps, width,
            [[x]], [(fsdp * tokens, 0, fsdp * tokens)], after=after,
        )
        products = products.reshape(fsdp * tokens, tp_size, piece).swapaxes(0, 1)
        mine = lax.psum_scatter(products, "tp", scatter_dimension=0, tiled=True)[0]
        mine = lax.psum_scatter(mine, "fsdp", scatter_dimension=0, tiled=True)
        out = turn(cosine, sine_part, [(mine, 0)], chunk * piece, share, out)
        after = (mine,)
    return out


def solution(mesh):
    fsdp, tp = mesh.shape["fsdp"], mesh.shape["tp"]
    if (fsdp, tp) == (4, 4):
        shards = line_shards
    else:
        shards = functools.partial(any_shards, fsdp, tp)
    placed = (
        P(("rep", "fsdp"), None),
        P(("rep", "fsdp", "tp"), None),
        P(("rep", "fsdp", "tp"), None),
        P("rep", None),
        P("rep"),
        P(("rep", "fsdp")),
    )
    return jax.shard_map(
        shards, mesh=mesh, in_specs=placed, out_specs=P(("rep", "fsdp"), "tp"), check_vma=False
    )
```

```python
import functools
import math

import jax
import jax.numpy as jnp
from jax import lax
from jax.experimental import pallas as pl
from jax.experimental.pallas import tpu as pltpu
from jax.sharding import PartitionSpec as P

HEAD = 128
BLOCK = 128
PIECES = 4
TILE = 512


norm_epsilon = 1e-05
scale_epsilon = 1e-06
code_limit = 15.0
adapter_scale = 2.0
rope_theta = 500000.0
rope_factor = 8.0
low_factor = 1.0
high_factor = 4.0
initial_context = 8192.0
feature_scale = 1024.0

ANY = pl.BlockSpec(memory_space=pl.ANY)


def params(mebibytes):
    return pltpu.CompilerParams(vmem_limit_bytes=mebibytes << 20)


def cost(flops, nbytes):
    return pl.CostEstimate(flops=int(flops), bytes_accessed=int(nbytes), transcendentals=0)


def like(shape, dtype=jnp.bfloat16):
    return jax.ShapeDtypeStruct(shape, dtype)


def frequencies(positions):
    pair_index = jnp.arange(HEAD // 2, dtype=jnp.float32)
    inverse = jnp.exp(pair_index * (-2.0 * math.log(rope_theta) / HEAD))
    wavelength = 2.0 * math.pi / inverse
    blend = (initial_context / wavelength - low_factor) / (high_factor - low_factor)
    middle = (1.0 - blend) * inverse / rope_factor + blend * inverse
    adjusted = jnp.where(
        wavelength < initial_context / high_factor,
        inverse,
        jnp.where(wavelength > initial_context / low_factor, inverse / rope_factor, middle),
    )
    angles = positions.astype(jnp.float32)[:, None] * adjusted[None, :]
    return (jnp.cos(angles), jnp.sin(angles))


def turn_tables(hidden, positions):
    values = hidden.astype(jnp.float32)
    mean_square = jnp.mean(values * values, axis=1, keepdims=True)
    factor = lax.rsqrt(mean_square + norm_epsilon) * (1.0 / feature_scale)
    cosine, sine_part = frequencies(positions)
    return (
        jnp.concatenate([cosine, cosine], axis=1) * factor,
        jnp.concatenate([-sine_part, sine_part], axis=1) * factor,
    )


def pick_kernel(table, *refs):
    count = len(refs) // 3
    for i in range(count):
        values, gain, out = refs[i], refs[count + i], refs[2 * count + i]
        scaled = values[...].astype(jnp.float32) * (gain[...].astype(jnp.float32) * feature_scale)
        out[...] = scaled.astype(jnp.bfloat16)


def pick(hidden, norm_gain, table, count, width):
    tokens = hidden.shape[0]

    def spec(rows, i):
        return pl.BlockSpec((rows, width), lambda step, table: (0, table[i]))

    return pl.pallas_call(
        pick_kernel,
        grid_spec=pltpu.PrefetchScalarGridSpec(
            num_scalar_prefetch=1,
            grid=(1,),
            in_specs=[spec(tokens, i) for i in range(count)] + [spec(1, i) for i in range(count)],
            out_specs=[pl.BlockSpec((tokens, width), lambda step, table: (0, 0))] * count,
        ),
        out_shape=[like((tokens, width))] * count,
        compiler_params=params(12),
        name="pick_features",
    )(table, *([hidden] * count), *([norm_gain] * count))


def scales_of(largest):
    ratio = (largest + scale_epsilon) / code_limit
    scale = jnp.exp2(jnp.ceil(jnp.log2(ratio))).astype(jnp.bfloat16).astype(jnp.float32)
    scale = jnp.where(ratio > scale, scale * 2.0, scale)
    return jnp.where(ratio <= scale * 0.5, scale * 0.5, scale)


def quantize_tile(base, down, up, weight, first, merged, scale_scratch):
    rows, width = base.shape
    row_blocks = rows // BLOCK
    first_block = first // BLOCK
    tops = []
    for i in range(row_blocks):
        block_rows = pl.ds(i * BLOCK, BLOCK)
        here = pl.ds(first + i * BLOCK, BLOCK)
        low_rank = jnp.dot(down[here, :], up[...], preferred_element_type=jnp.float32)
        total = base[block_rows, :].astype(jnp.float32) + low_rank
        merged[here, :] = total
        tops.append(jnp.max(jnp.abs(total), axis=0, keepdims=True))
    top = jnp.concatenate(tops, axis=0)
    blocks = pl.ds(first_block, row_blocks)
    for j in range(width // BLOCK):
        cols = slice(j * BLOCK, (j + 1) * BLOCK)
        largest = jnp.max(top[:, cols], axis=1, keepdims=True)
        scale = scales_of(jnp.broadcast_to(largest, (row_blocks, BLOCK)))
        scale_scratch[0, blocks, cols] = scale
        scale_scratch[1, blocks, cols] = 1.0 / scale
    for i in range(row_blocks):
        here = pl.ds(first + i * BLOCK, BLOCK)
        scale = scale_scratch[0, pl.ds(first_block + i, 1), :]
        inverse = scale_scratch[1, pl.ds(first_block + i, 1), :]
        codes = jnp.floor(merged[here, :] * inverse + 0.5)
        weight[here, :] = codes.astype(jnp.bfloat16) * scale.astype(jnp.bfloat16)


def gather_features(pieces, x):
    @pl.when(pl.program_id(0) == 0)
    def _():
        row = 0
        for line in pieces:
            col = 0
            for piece in line:
                x[row : row + piece.shape[0], col : col + piece.shape[1]] = piece[...]
                col += piece.shape[1]
            row += line[0].shape[0]


def store_rows(product, outs):
    first = 0
    for out in outs:
        out[...] = product[first : first + out.shape[0], :].astype(jnp.bfloat16)
        first += out.shape[0]


def split_lines(refs, shape):
    lines = []
    for length in shape:
        lines.append(refs[:length])
        refs = refs[length:]
    return lines, refs


def pass_kernel(sources, shape, late, after, keep, outs, carry, table, *refs):
    if carry:
        end = len(refs) - (3 if keep else 4)
        for k in range(carry):
            refs[end - carry + k][...] = refs[k][...]
        refs = refs[carry : end - carry] + refs[end:]
    bases, refs = refs[:sources], refs[sources:]
    (down, up), refs = refs[:2], refs[2:]
    kept, refs = (refs[0], refs[1:]) if late else (None, refs)
    lines, refs = split_lines(refs, shape)
    refs = refs[after:]
    place = 0 if keep else outs
    weight, refs = refs[place], refs[:place] + refs[place + 1 :]
    outs, (x, merged, scale_scratch) = refs[:outs], refs[outs:]
    if lines:
        gather_features(lines, x)
    products = []
    if late:
        tokens = lines[-1][0].shape[0]
        last = x[x.shape[0] - tokens :, :]
        products.append(jnp.dot(last, kept[...], preferred_element_type=jnp.float32))
    rows = bases[0].shape[0]
    for i, base in enumerate(bases):
        quantize_tile(base, down, up, weight, i * rows, merged, scale_scratch)
    if lines:
        products.append(jnp.dot(x[...], weight[...], preferred_element_type=jnp.float32))
        store_rows(jnp.concatenate(products, axis=0) if late else products[0], outs)


def row_outs(out_rows, steps, width):
    def spec(count, block):
        return pl.BlockSpec((count, width), lambda i, *_: (block, i))

    shapes = [like((total, steps * width)) for _, _, total in out_rows]
    return shapes, [spec(count, block) for count, block, _ in out_rows]


def merge_pass(
    bases, down, up, table, steps, width, lines=(), out_rows=(), kept=None, keep=False, carry=None,
    onto=None, after=(),
):
    rows = bases[0][0].shape[0]
    depth, rank = down.shape
    tokens = sum(line[0].shape[0] for line in lines)

    def fixed(shape):
        return pl.BlockSpec(shape, lambda i, table: (0, 0))

    def tile(height, place):
        if place is None:
            return pl.BlockSpec((height, width), lambda i, table: (0, table[i]))
        return pl.BlockSpec((height, width), lambda i, table: (0, place + i))

    operands = [base for base, _ in bases] + [down, up]
    in_specs = [tile(rows, place) for _, place in bases] + [fixed(down.shape), tile(rank, None)]
    if kept is not None:
        operands.append(kept)
        in_specs.append(tile(depth, 0))
    for line in lines:
        operands += line
        in_specs += [fixed(piece.shape) for piece in line]
    if onto is not None:
        after = (onto, *after)
    operands += after
    in_specs += [ANY] * len(after)
    out_shape, out_specs = row_outs(out_rows, steps, width)
    carried = 0
    if carry is not None:
        values, span, carried = carry
        block = (values.shape[0], span)

        def carry_spec(k):
            return pl.BlockSpec(block, lambda i, table: (0, table[steps + k * steps + i]))

        operands = [values] * carried + operands
        in_specs = [carry_spec(k) for k in range(carried)] + in_specs
    scratch = [
        pltpu.VMEM((max(tokens, 16), depth), jnp.bfloat16),
        pltpu.VMEM((depth, width), jnp.float32),
        pltpu.VMEM((2, depth // BLOCK, width), jnp.float32),
    ]
    if keep:
        out_shape.insert(0, pltpu.HBM((depth, steps * width), jnp.bfloat16))
        out_specs.insert(0, tile(depth, 0))
    else:
        scratch.insert(0, pltpu.VMEM((depth, width), jnp.bfloat16))
    if carry is not None:
        out_shape += [pltpu.HBM((block[0], steps * span), jnp.bfloat16)] * carried
        out_specs += [pl.BlockSpec(block, lambda i, table: (0, i))] * carried
    return pl.pallas_call(
        functools.partial(
            pass_kernel, len(bases), [len(line) for line in lines], kept is not None, len(after),
            keep, len(out_rows), carried,
        ),
        grid_spec=pltpu.PrefetchScalarGridSpec(
            num_scalar_prefetch=1,
            grid=(steps,),
            in_specs=in_specs,
            out_specs=out_specs,
            scratch_shapes=scratch,
        ),
        out_shape=out_shape,
        input_output_aliases={} if onto is None else {1 + len(operands) - len(after): 0},
        cost_estimate=cost(2 * tokens * depth * steps * width, 4 * depth * steps * width),
        compiler_params=params(42 if carried else 28),
        name="merge_pass",
    )(table, *operands)


def take_kernel(table, values, *refs):
    refs[-1][...] = values[...]


def take_tiles(values, table, steps, width, after=()):
    rows = values.shape[0]
    return pl.pallas_call(
        take_kernel,
        grid_spec=pltpu.PrefetchScalarGridSpec(
            num_scalar_prefetch=1,
            grid=(steps,),
            in_specs=[pl.BlockSpec((rows, width), lambda i, table: (0, table[i]))]
            + [ANY] * len(after),
            out_specs=pl.BlockSpec((rows, width), lambda i, table: (0, i)),
        ),
        out_shape=pltpu.HBM((rows, steps * width), jnp.bfloat16),
        compiler_params=params(40),
        name="take_tiles",
    )(table, values, *after)


def turn_kernel(count, cosine, sine_part, *refs):
    out = refs[-1]
    for j in range(out.shape[1] // HEAD):
        cols = slice(j * HEAD, (j + 1) * HEAD)
        total = refs[0][:, cols].astype(jnp.float32)
        for term in refs[1:count]:
            total = total + term[:, cols].astype(jnp.float32)
        swapped = pltpu.roll(total, HEAD // 2, 1)
        turned = total * cosine[...] + swapped * sine_part[...]
        out[:, cols] = turned.astype(jnp.bfloat16)


def turn(cosine, sine_part, terms, place, places, into, after=()):
    tokens = cosine.shape[0]
    columns = terms[0][0].shape[1]
    width = math.gcd(columns, place) if place else columns
    table = pl.BlockSpec((tokens, HEAD), lambda i: (0, 0))

    def term_spec(block):
        return pl.BlockSpec((tokens, width), lambda i: (block, i))

    extra = [] if into is None else [into]
    count = len(terms)
    return pl.pallas_call(
        functools.partial(turn_kernel, count),
        grid=(columns // width,),
        in_specs=[table] * 2 + [term_spec(block) for _, block in terms]
        + [ANY] * (len(extra) + len(after)),
        out_specs=pl.BlockSpec((tokens, width), lambda i: (0, place // width + i)),
        out_shape=like((tokens, places)),
        input_output_aliases={2 + count: 0} if extra else {},
        compiler_params=params(12),
        name="turn",
    )(cosine, sine_part, *[term for term, _ in terms], *extra, *after)


def add_kernel(count, *refs):
    total = refs[0][...].astype(jnp.float32)
    for term in refs[1:count]:
        total = total + term[...].astype(jnp.float32)
    refs[-1][...] = total.astype(jnp.bfloat16)


def added(terms, rows, after=()):
    columns = terms[0][0].shape[1]
    width = tile_width(columns, 512)

    def term_spec(block):
        return pl.BlockSpec((rows, width), lambda i: (block, i))

    return pl.pallas_call(
        functools.partial(add_kernel, len(terms)),
        grid=(columns // width,),
        in_specs=[term_spec(block) for _, block in terms] + [ANY] * len(after),
        out_specs=term_spec(0),
        out_shape=like((rows, columns)),
        compiler_params=params(12),
        name="add_terms",
    )(*[term for term, _ in terms], *after)


def tile_width(columns, most):
    width = min(columns, most)
    while columns % width:
        width //= 2
    return width


def line_shards(hidden, base, down, up, norm_gain, positions):
    tp = lax.axis_index("tp")
    z = lax.axis_index("fsdp")
    rows, all_columns = base.shape
    tokens = hidden.shape[0]
    quarter = all_columns // 4
    other_core, other_chip, other_both = tp ^ 1, tp ^ 2, tp ^ 3

    def over(axis, distance):
        return functools.partial(
            lax.ppermute, axis_name=axis, perm=[(i, i ^ distance) for i in range(4)]
        )

    over_core, over_y = over("tp", 1), over("tp", 2)
    over_z1, over_z2 = over("fsdp", 1), over("fsdp", 2)

    piece = quarter // PIECES
    width = tile_width(piece, min(TILE, piece // 2))
    steps = piece // width

    def tiles(*places):
        offsets = jnp.arange(steps, dtype=jnp.int32)
        starts = [owner * (quarter // width) + i * steps for owner, i in places]
        return jnp.concatenate([start + offsets for start in starts]).astype(jnp.int32)

    blocks = [(z ^ d) * 4 + tp for d in range(4)] + [z * 4 + other_core]
    own_x, p1, p2, p3, own_other = pick(
        hidden, norm_gain[None, :], jnp.stack(blocks).astype(jnp.int32), 5, rows
    )
    x1, x2, x3 = over("fsdp", 1)(p1), over("fsdp", 2)(p2), over("fsdp", 3)(p3)
    first_lines = [[x1, over_core(x1)], [x3, over_core(x3)], [own_x, own_other]]

    down2 = jnp.concatenate([down, over_core(down)], axis=0)
    up2 = up * jnp.bfloat16(adapter_scale)

    def spans(names, count):
        span = min(piece, piece * len(names) // count)
        each = piece // span
        owners = [(other_both if kind == "y" else other_core) for kind, _ in names]
        firsts = [(owner * PIECES + i) * each for owner, (_, i) in zip(owners, names)]
        blocks = [first + k for first in firsts for k in range(each)]
        return jnp.stack(blocks).astype(jnp.int32), span

    received = {}

    def send(taken, names):
        arrived = over_core(taken)
        for k, name in enumerate(names):
            received[name] = (arrived, k * steps)

    def take(names, after):
        table, span = spans(names, len(names))
        taken = take_tiles(base, table, len(names), span, after)
        send(taken, names)
        return taken

    taken = take([("y", 0)], (own_x,))
    taken = take([("y", 1), ("own", 0), ("y", 2)], (taken, down2))

    def run_pass(owner, i, kind, carried, **options):
        table = tiles((owner, i))
        carry = None
        if carried:
            blocks, span = spans(sum(carried, []), steps * len(carried))
            table = jnp.concatenate([table, blocks])
            carry = (base, span, len(carried))
        outs = merge_pass(
            [(base, None), received[kind, i]], down2, up2, table, steps, width, carry=carry, **options,
        )
        if carried:
            outs, taken = outs[: -len(carried)], outs[-len(carried) :]
            for value, names in zip(taken, carried):
                send(value, names)
        return outs

    first_rows = [(2 * tokens, 0, 2 * tokens), (tokens, 0, 2 * tokens)]
    second_rows = [(tokens, 1, 2 * tokens), (2 * tokens, 0, 2 * tokens)] + [(tokens, 0, tokens)] * 2
    weights, halves, far_y, mid_y = {}, {}, {}, {}
    near, own, far, near_z, far_z = {}, {}, {}, {}, {}

    def first(i, after, carried=()):
        weights[i], value, halves[i] = run_pass(
            other_chip, i, "y", carried, lines=first_lines, out_rows=first_rows, keep=True, after=after
        )
        far_y[i] = over_y(value)
        return value

    def second(i, after):
        half, near[i], own[i], far[i] = run_pass(
            tp, i, "own", (), lines=all_lines, out_rows=second_rows, kept=weights[i],
            onto=halves[i], after=after,
        )
        mid_y[i] = over_y(half)
        return half

    def to_z1(i, after):
        operand = added([(near[i], 0), (far_y[i], 0)], 2 * tokens, after)
        near_z[i] = over_z1(operand)
        return operand

    def to_z2(i, after):
        operand = added([(far[i], 0), (mid_y[i], 1), (near_z[i], 1)], tokens, after)
        far_z[i] = over_z2(operand)
        return operand

    def finish(i, out, after):
        terms = [(own[i], 0), (mid_y[i], 0), (near_z[i], 0), (far_z[i], 0)]
        return turn(cosine, sine_part, terms, i * piece, quarter, out, after)

    done = first(0, (taken,), [[("own", 1), ("y", 3)], [("own", 2), ("own", 3)]])
    k1 = first(1, (done,))
    done = first(2, (k1,))
    all_lines = [*first_lines, [x2, over_core(lax.optimization_barrier((x2, k1))[0])]]
    done = second(0, (done, received["own", 1][0], received["own", 2][0], far_y[0], far_y[1]))
    done = to_z1(0, (done,))
    done = second(1, (done, far_y[1]))
    done = to_z1(1, (done,))
    done = second(2, (done, far_y[2]))
    done = to_z2(0, (done,))
    done = to_z1(2, (done,))
    done = first(3, (done, near_z[1]))
    cosine, sine_part = turn_tables(lax.optimization_barrier((hidden, done))[0], positions)
    out = finish(0, None, (done,))
    done = to_z2(1, (out,))
    done = second(3, (done,))
    done = to_z2(2, (done,))
    out = finish(1, out, (done,))
    done = to_z1(3, (out,))
    done = to_z2(3, (done,))
    out = finish(2, out, (done,))
    return finish(3, out, ())


def any_shards(fsdp, tp_size, hidden, base, down, up, norm_gain, positions):
    tp = lax.axis_index("tp")
    rows, all_columns = base.shape
    tokens = hidden.shape[0]
    share = all_columns // tp_size
    chunks = max(1, share // 256)
    piece = share // chunks
    width = tile_width(piece, TILE)
    steps = piece // width

    blocks = (jnp.arange(fsdp) * tp_size + tp).astype(jnp.int32)
    picked = pick(hidden, norm_gain[None, :], blocks, fsdp, rows)
    x = lax.all_to_all(jnp.stack(picked), "fsdp", 0, 0, tiled=True)
    x = x.reshape(fsdp * tokens, rows)
    up2 = up * jnp.bfloat16(adapter_scale)
    cosine, sine_part = turn_tables(hidden, positions)
    out = None
    after = ()
    for chunk in range(chunks):
        owners = jnp.arange(tp_size, dtype=jnp.int32)[:, None] * (share // width)
        offsets = jnp.arange(steps, dtype=jnp.int32)[None, :] + chunk * steps
        (products,) = merge_pass(
            [(base, None)], down, up2, (owners + offsets).reshape(-1), tp_size * steps, width,
            [[x]], [(fsdp * tokens, 0, fsdp * tokens)], after=after,
        )
        products = products.reshape(fsdp * tokens, tp_size, piece).swapaxes(0, 1)
        mine = lax.psum_scatter(products, "tp", scatter_dimension=0, tiled=True)[0]
        mine = lax.psum_scatter(mine, "fsdp", scatter_dimension=0, tiled=True)
        out = turn(cosine, sine_part, [(mine, 0)], chunk * piece, share, out)
        after = (mine,)
    return out


def solution(mesh):
    fsdp, tp = mesh.shape["fsdp"], mesh.shape["tp"]
    if (fsdp, tp) == (4, 4):
        shards = line_shards
    else:
        shards = functools.partial(any_shards, fsdp, tp)
    placed = (
        P(("rep", "fsdp"), None),
        P(("rep", "fsdp", "tp"), None),
        P(("rep", "fsdp", "tp"), None),
        P("rep", None),
        P("rep"),
        P(("rep", "fsdp")),
    )
    return jax.shard_map(
        shards, mesh=mesh, in_specs=placed, out_specs=P(("rep", "fsdp"), "tp"), check_vma=False
    )
```

```python
import functools
import math

import jax
import jax.numpy as jnp
from jax import lax
from jax.experimental import pallas as pl
from jax.experimental.pallas import tpu as pltpu
from jax.sharding import PartitionSpec as P

HEAD = 128
BLOCK = 128
PIECES = 4
TILE = 512


norm_epsilon = 1e-05
scale_epsilon = 1e-06
code_limit = 15.0
adapter_scale = 2.0
rope_theta = 500000.0
rope_factor = 8.0
low_factor = 1.0
high_factor = 4.0
initial_context = 8192.0
feature_scale = 1024.0

ANY = pl.BlockSpec(memory_space=pl.ANY)


def params(mebibytes):
    return pltpu.CompilerParams(vmem_limit_bytes=mebibytes << 20)


def cost(flops, nbytes):
    return pl.CostEstimate(flops=int(flops), bytes_accessed=int(nbytes), transcendentals=0)


def like(shape, dtype=jnp.bfloat16):
    return jax.ShapeDtypeStruct(shape, dtype)


def frequencies(positions):
    pair_index = jnp.arange(HEAD // 2, dtype=jnp.float32)
    inverse = jnp.exp(pair_index * (-2.0 * math.log(rope_theta) / HEAD))
    wavelength = 2.0 * math.pi / inverse
    blend = (initial_context / wavelength - low_factor) / (high_factor - low_factor)
    middle = (1.0 - blend) * inverse / rope_factor + blend * inverse
    adjusted = jnp.where(
        wavelength < initial_context / high_factor,
        inverse,
        jnp.where(wavelength > initial_context / low_factor, inverse / rope_factor, middle),
    )
    angles = positions.astype(jnp.float32)[:, None] * adjusted[None, :]
    return (jnp.cos(angles), jnp.sin(angles))


def turn_tables(hidden, positions):
    values = hidden.astype(jnp.float32)
    mean_square = jnp.mean(values * values, axis=1, keepdims=True)
    factor = lax.rsqrt(mean_square + norm_epsilon) * (1.0 / feature_scale)
    cosine, sine_part = frequencies(positions)
    return (
        jnp.concatenate([cosine, cosine], axis=1) * factor,
        jnp.concatenate([-sine_part, sine_part], axis=1) * factor,
    )


def pick_kernel(table, *refs):
    count = len(refs) // 3
    for i in range(count):
        values, gain, out = refs[i], refs[count + i], refs[2 * count + i]
        scaled = values[...].astype(jnp.float32) * (gain[...].astype(jnp.float32) * feature_scale)
        out[...] = scaled.astype(jnp.bfloat16)


def pick(hidden, norm_gain, table, count, width):
    tokens = hidden.shape[0]

    def spec(rows, i):
        return pl.BlockSpec((rows, width), lambda step, table: (0, table[i]))

    return pl.pallas_call(
        pick_kernel,
        grid_spec=pltpu.PrefetchScalarGridSpec(
            num_scalar_prefetch=1,
            grid=(1,),
            in_specs=[spec(tokens, i) for i in range(count)] + [spec(1, i) for i in range(count)],
            out_specs=[pl.BlockSpec((tokens, width), lambda step, table: (0, 0))] * count,
        ),
        out_shape=[like((tokens, width))] * count,
        compiler_params=params(12),
        name="pick_features",
    )(table, *([hidden] * count), *([norm_gain] * count))


def scales_of(largest):
    ratio = (largest + scale_epsilon) / code_limit
    scale = jnp.exp2(jnp.ceil(jnp.log2(ratio))).astype(jnp.bfloat16).astype(jnp.float32)
    scale = jnp.where(ratio > scale, scale * 2.0, scale)
    return jnp.where(ratio <= scale * 0.5, scale * 0.5, scale)


def quantize_tile(base, down, up, weight, first, merged, scale_scratch):
    rows, width = base.shape
    row_blocks = rows // BLOCK
    first_block = first // BLOCK
    tops = []
    for i in range(row_blocks):
        block_rows = pl.ds(i * BLOCK, BLOCK)
        here = pl.ds(first + i * BLOCK, BLOCK)
        low_rank = jnp.dot(down[here, :], up[...], preferred_element_type=jnp.float32)
        total = base[block_rows, :].astype(jnp.float32) + low_rank
        merged[here, :] = total
        tops.append(jnp.max(jnp.abs(total), axis=0, keepdims=True))
    top = jnp.concatenate(tops, axis=0)
    blocks = pl.ds(first_block, row_blocks)
    for j in range(width // BLOCK):
        cols = slice(j * BLOCK, (j + 1) * BLOCK)
        largest = jnp.max(top[:, cols], axis=1, keepdims=True)
        scale = scales_of(jnp.broadcast_to(largest, (row_blocks, BLOCK)))
        scale_scratch[0, blocks, cols] = scale
        scale_scratch[1, blocks, cols] = 1.0 / scale
    for i in range(row_blocks):
        here = pl.ds(first + i * BLOCK, BLOCK)
        scale = scale_scratch[0, pl.ds(first_block + i, 1), :]
        inverse = scale_scratch[1, pl.ds(first_block + i, 1), :]
        codes = jnp.floor(merged[here, :] * inverse + 0.5)
        weight[here, :] = codes.astype(jnp.bfloat16) * scale.astype(jnp.bfloat16)


def gather_features(pieces, x):
    @pl.when(pl.program_id(0) == 0)
    def _():
        row = 0
        for line in pieces:
            col = 0
            for piece in line:
                x[row : row + piece.shape[0], col : col + piece.shape[1]] = piece[...]
                col += piece.shape[1]
            row += line[0].shape[0]


def store_rows(product, outs):
    first = 0
    for out in outs:
        out[...] = product[first : first + out.shape[0], :].astype(jnp.bfloat16)
        first += out.shape[0]


def split_lines(refs, shape):
    lines = []
    for length in shape:
        lines.append(refs[:length])
        refs = refs[length:]
    return lines, refs


def pass_kernel(sources, shape, late, after, keep, outs, carry, table, *refs):
    if carry:
        end = len(refs) - (3 if keep else 4)
        for k in range(carry):
            refs[end - carry + k][...] = refs[k][...]
        refs = refs[carry : end - carry] + refs[end:]
    bases, refs = refs[:sources], refs[sources:]
    (down, up), refs = refs[:2], refs[2:]
    kept, refs = (refs[0], refs[1:]) if late else (None, refs)
    lines, refs = split_lines(refs, shape)
    refs = refs[after:]
    place = 0 if keep else outs
    weight, refs = refs[place], refs[:place] + refs[place + 1 :]
    outs, (x, merged, scale_scratch) = refs[:outs], refs[outs:]
    if lines:
        gather_features(lines, x)
    products = []
    if late:
        tokens = lines[-1][0].shape[0]
        last = x[x.shape[0] - tokens :, :]
        products.append(jnp.dot(last, kept[...], preferred_element_type=jnp.float32))
    rows = bases[0].shape[0]
    for i, base in enumerate(bases):
        quantize_tile(base, down, up, weight, i * rows, merged, scale_scratch)
    if lines:
        products.append(jnp.dot(x[...], weight[...], preferred_element_type=jnp.float32))
        store_rows(jnp.concatenate(products, axis=0) if late else products[0], outs)


def row_outs(out_rows, steps, width):
    def spec(count, block):
        return pl.BlockSpec((count, width), lambda i, *_: (block, i))

    shapes = [like((total, steps * width)) for _, _, total in out_rows]
    return shapes, [spec(count, block) for count, block, _ in out_rows]


def merge_pass(
    bases, down, up, table, steps, width, lines=(), out_rows=(), kept=None, keep=False, carry=None,
    onto=None, after=(),
):
    rows = bases[0][0].shape[0]
    depth, rank = down.shape
    tokens = sum(line[0].shape[0] for line in lines)

    def fixed(shape):
        return pl.BlockSpec(shape, lambda i, table: (0, 0))

    def tile(height, place):
        if place is None:
            return pl.BlockSpec((height, width), lambda i, table: (0, table[i]))
        return pl.BlockSpec((height, width), lambda i, table: (0, place + i))

    operands = [base for base, _ in bases] + [down, up]
    in_specs = [tile(rows, place) for _, place in bases] + [fixed(down.shape), tile(rank, None)]
    if kept is not None:
        operands.append(kept)
        in_specs.append(tile(depth, 0))
    for line in lines:
        operands += line
        in_specs += [fixed(piece.shape) for piece in line]
    if onto is not None:
        after = (onto, *after)
    operands += after
    in_specs += [ANY] * len(after)
    out_shape, out_specs = row_outs(out_rows, steps, width)
    carried = 0
    if carry is not None:
        values, span, carried = carry
        block = (values.shape[0], span)

        def carry_spec(k):
            return pl.BlockSpec(block, lambda i, table: (0, table[steps + k * steps + i]))

        operands = [values] * carried + operands
        in_specs = [carry_spec(k) for k in range(carried)] + in_specs
    scratch = [
        pltpu.VMEM((max(tokens, 16), depth), jnp.bfloat16),
        pltpu.VMEM((depth, width), jnp.float32),
        pltpu.VMEM((2, depth // BLOCK, width), jnp.float32),
    ]
    if keep:
        out_shape.insert(0, pltpu.HBM((depth, steps * width), jnp.bfloat16))
        out_specs.insert(0, tile(depth, 0))
    else:
        scratch.insert(0, pltpu.VMEM((depth, width), jnp.bfloat16))
    if carry is not None:
        out_shape += [pltpu.HBM((block[0], steps * span), jnp.bfloat16)] * carried
        out_specs += [pl.BlockSpec(block, lambda i, table: (0, i))] * carried
    return pl.pallas_call(
        functools.partial(
            pass_kernel, len(bases), [len(line) for line in lines], kept is not None, len(after),
            keep, len(out_rows), carried,
        ),
        grid_spec=pltpu.PrefetchScalarGridSpec(
            num_scalar_prefetch=1,
            grid=(steps,),
            in_specs=in_specs,
            out_specs=out_specs,
            scratch_shapes=scratch,
        ),
        out_shape=out_shape,
        input_output_aliases={} if onto is None else {1 + len(operands) - len(after): 0},
        cost_estimate=cost(2 * tokens * depth * steps * width, 4 * depth * steps * width),
        compiler_params=params(42 if carried else 28),
        name="merge_pass",
    )(table, *operands)


def take_kernel(table, values, *refs):
    refs[-1][...] = values[...]


def take_tiles(values, table, steps, width, after=()):
    rows = values.shape[0]
    return pl.pallas_call(
        take_kernel,
        grid_spec=pltpu.PrefetchScalarGridSpec(
            num_scalar_prefetch=1,
            grid=(steps,),
            in_specs=[pl.BlockSpec((rows, width), lambda i, table: (0, table[i]))]
            + [ANY] * len(after),
            out_specs=pl.BlockSpec((rows, width), lambda i, table: (0, i)),
        ),
        out_shape=pltpu.HBM((rows, steps * width), jnp.bfloat16),
        compiler_params=params(40),
        name="take_tiles",
    )(table, values, *after)


def turn_kernel(count, cosine, sine_part, *refs):
    out = refs[-1]
    for j in range(out.shape[1] // HEAD):
        cols = slice(j * HEAD, (j + 1) * HEAD)
        total = refs[0][:, cols].astype(jnp.float32)
        for term in refs[1:count]:
            total = total + term[:, cols].astype(jnp.float32)
        swapped = pltpu.roll(total, HEAD // 2, 1)
        turned = total * cosine[...] + swapped * sine_part[...]
        out[:, cols] = turned.astype(jnp.bfloat16)


def turn(cosine, sine_part, terms, place, places, into, after=()):
    tokens = cosine.shape[0]
    columns = terms[0][0].shape[1]
    width = math.gcd(columns, place) if place else columns
    table = pl.BlockSpec((tokens, HEAD), lambda i: (0, 0))

    def term_spec(block):
        return pl.BlockSpec((tokens, width), lambda i: (block, i))

    extra = [] if into is None else [into]
    count = len(terms)
    return pl.pallas_call(
        functools.partial(turn_kernel, count),
        grid=(columns // width,),
        in_specs=[table] * 2 + [term_spec(block) for _, block in terms]
        + [ANY] * (len(extra) + len(after)),
        out_specs=pl.BlockSpec((tokens, width), lambda i: (0, place // width + i)),
        out_shape=like((tokens, places)),
        input_output_aliases={2 + count: 0} if extra else {},
        compiler_params=params(12),
        name="turn",
    )(cosine, sine_part, *[term for term, _ in terms], *extra, *after)


def add_kernel(count, *refs):
    total = refs[0][...].astype(jnp.float32)
    for term in refs[1:count]:
        total = total + term[...].astype(jnp.float32)
    refs[-1][...] = total.astype(jnp.bfloat16)


def added(terms, rows, after=()):
    columns = terms[0][0].shape[1]
    width = tile_width(columns, 512)

    def term_spec(block):
        return pl.BlockSpec((rows, width), lambda i: (block, i))

    return pl.pallas_call(
        functools.partial(add_kernel, len(terms)),
        grid=(columns // width,),
        in_specs=[term_spec(block) for _, block in terms] + [ANY] * len(after),
        out_specs=term_spec(0),
        out_shape=like((rows, columns)),
        compiler_params=params(12),
        name="add_terms",
    )(*[term for term, _ in terms], *after)


def tile_width(columns, most):
    width = min(columns, most)
    while columns % width:
        width //= 2
    return width


def line_shards(hidden, base, down, up, norm_gain, positions):
    tp = lax.axis_index("tp")
    z = lax.axis_index("fsdp")
    rows, all_columns = base.shape
    tokens = hidden.shape[0]
    quarter = all_columns // 4
    other_core, other_chip, other_both = tp ^ 1, tp ^ 2, tp ^ 3

    def over(axis, distance):
        return functools.partial(
            lax.ppermute, axis_name=axis, perm=[(i, i ^ distance) for i in range(4)]
        )

    over_core, over_y = over("tp", 1), over("tp", 2)
    over_z1, over_z2 = over("fsdp", 1), over("fsdp", 2)

    piece = quarter // PIECES
    width = tile_width(piece, min(TILE, piece // 2))
    steps = piece // width

    def tiles(*places):
        offsets = jnp.arange(steps, dtype=jnp.int32)
        starts = [owner * (quarter // width) + i * steps for owner, i in places]
        return jnp.concatenate([start + offsets for start in starts]).astype(jnp.int32)

    blocks = [(z ^ d) * 4 + tp for d in range(4)] + [z * 4 + other_core]
    own_x, p1, p2, p3, own_other = pick(
        hidden, norm_gain[None, :], jnp.stack(blocks).astype(jnp.int32), 5, rows
    )
    x1, x2, x3 = over("fsdp", 1)(p1), over("fsdp", 2)(p2), over("fsdp", 3)(p3)
    first_lines = [[x1, over_core(x1)], [x3, over_core(x3)], [own_x, own_other]]

    down2 = jnp.concatenate([down, over_core(down)], axis=0)
    up2 = up * jnp.bfloat16(adapter_scale)

    def spans(names, count):
        span = min(piece, piece * len(names) // count)
        each = piece // span
        owners = [(other_both if kind == "y" else other_core) for kind, _ in names]
        firsts = [(owner * PIECES + i) * each for owner, (_, i) in zip(owners, names)]
        blocks = [first + k for first in firsts for k in range(each)]
        return jnp.stack(blocks).astype(jnp.int32), span

    received = {}

    def send(taken, names):
        arrived = over_core(taken)
        for k, name in enumerate(names):
            received[name] = (arrived, k * steps)

    def take(names, after):
        table, span = spans(names, len(names))
        taken = take_tiles(base, table, len(names), span, after)
        send(taken, names)
        return taken

    taken = take([("y", 0)], (own_x,))
    taken = take([("y", 1), ("own", 0), ("y", 2)], (taken, down2))

    def run_pass(owner, i, kind, carried, **options):
        table = tiles((owner, i))
        carry = None
        if carried:
            blocks, span = spans(sum(carried, []), steps * len(carried))
            table = jnp.concatenate([table, blocks])
            carry = (base, span, len(carried))
        outs = merge_pass(
            [(base, None), received[kind, i]], down2, up2, table, steps, width, carry=carry, **options,
        )
        if carried:
            outs, taken = outs[: -len(carried)], outs[-len(carried) :]
            for value, names in zip(taken, carried):
                send(value, names)
        return outs

    first_rows = [(2 * tokens, 0, 2 * tokens), (tokens, 0, 2 * tokens)]
    second_rows = [(tokens, 1, 2 * tokens), (2 * tokens, 0, 2 * tokens)] + [(tokens, 0, tokens)] * 2
    weights, halves, far_y, mid_y = {}, {}, {}, {}
    near, own, far, near_z, far_z = {}, {}, {}, {}, {}

    def first(i, after, carried=()):
        weights[i], value, halves[i] = run_pass(
            other_chip, i, "y", carried, lines=first_lines, out_rows=first_rows, keep=True, after=after
        )
        far_y[i] = over_y(value)
        return value

    def second(i, after):
        half, near[i], own[i], far[i] = run_pass(
            tp, i, "own", (), lines=all_lines, out_rows=second_rows, kept=weights[i],
            onto=halves[i], after=after,
        )
        mid_y[i] = over_y(half)
        return half

    def to_z1(i, after):
        operand = added([(near[i], 0), (far_y[i], 0)], 2 * tokens, after)
        near_z[i] = over_z1(operand)
        return operand

    def to_z2(i, after):
        operand = added([(far[i], 0), (mid_y[i], 1), (near_z[i], 1)], tokens, after)
        far_z[i] = over_z2(operand)
        return operand

    def finish(i, out, after):
        terms = [(own[i], 0), (mid_y[i], 0), (near_z[i], 0), (far_z[i], 0)]
        return turn(cosine, sine_part, terms, i * piece, quarter, out, after)

    done = first(0, (taken,), [[("own", 1), ("y", 3)], [("own", 2), ("own", 3)]])
    k1 = first(1, (done,))
    done = first(2, (k1,))
    all_lines = [*first_lines, [x2, over_core(lax.optimization_barrier((x2, k1))[0])]]
    done = second(0, (done, received["own", 1][0], received["own", 2][0], far_y[0], far_y[1]))
    done = to_z1(0, (done,))
    done = second(1, (done, far_y[1]))
    done = to_z1(1, (done,))
    done = second(2, (done, far_y[2]))
    done = to_z2(0, (done,))
    done = to_z1(2, (done,))
    done = first(3, (done, near_z[1]))
    cosine, sine_part = turn_tables(lax.optimization_barrier((hidden, done))[0], positions)
    out = finish(0, None, (done,))
    done = to_z2(1, (out,))
    done = second(3, (done, near_z[2], mid_y[2]))
    out = finish(1, out, (done,))
    done = to_z1(3, (out,))
    done = to_z2(2, (done,))
    done = to_z2(3, (done,))
    out = finish(2, out, (done,))
    return finish(3, out, ())


def any_shards(fsdp, tp_size, hidden, base, down, up, norm_gain, positions):
    tp = lax.axis_index("tp")
    rows, all_columns = base.shape
    tokens = hidden.shape[0]
    share = all_columns // tp_size
    chunks = max(1, share // 256)
    piece = share // chunks
    width = tile_width(piece, TILE)
    steps = piece // width

    blocks = (jnp.arange(fsdp) * tp_size + tp).astype(jnp.int32)
    picked = pick(hidden, norm_gain[None, :], blocks, fsdp, rows)
    x = lax.all_to_all(jnp.stack(picked), "fsdp", 0, 0, tiled=True)
    x = x.reshape(fsdp * tokens, rows)
    up2 = up * jnp.bfloat16(adapter_scale)
    cosine, sine_part = turn_tables(hidden, positions)
    out = None
    after = ()
    for chunk in range(chunks):
        owners = jnp.arange(tp_size, dtype=jnp.int32)[:, None] * (share // width)
        offsets = jnp.arange(steps, dtype=jnp.int32)[None, :] + chunk * steps
        (products,) = merge_pass(
            [(base, None)], down, up2, (owners + offsets).reshape(-1), tp_size * steps, width,
            [[x]], [(fsdp * tokens, 0, fsdp * tokens)], after=after,
        )
        products = products.reshape(fsdp * tokens, tp_size, piece).swapaxes(0, 1)
        mine = lax.psum_scatter(products, "tp", scatter_dimension=0, tiled=True)[0]
        mine = lax.psum_scatter(mine, "fsdp", scatter_dimension=0, tiled=True)
        out = turn(cosine, sine_part, [(mine, 0)], chunk * piece, share, out)
        after = (mine,)
    return out


def solution(mesh):
    fsdp, tp = mesh.shape["fsdp"], mesh.shape["tp"]
    if (fsdp, tp) == (4, 4):
        shards = line_shards
    else:
        shards = functools.partial(any_shards, fsdp, tp)
    placed = (
        P(("rep", "fsdp"), None),
        P(("rep", "fsdp", "tp"), None),
        P(("rep", "fsdp", "tp"), None),
        P("rep", None),
        P("rep"),
        P(("rep", "fsdp")),
    )
    return jax.shard_map(
        shards, mesh=mesh, in_specs=placed, out_specs=P(("rep", "fsdp"), "tp"), check_vma=False
    )
```
